128 devices in a mesh: dev: 128 (over z, x, y, core).
Axes of the slice: x: 4, y: 4, z: 4, core: 2. Of those that a mesh axis runs over, the one named last changes fastest.
Arguments:
- features: bfloat16 [786432, 128], P('dev'), may hold values from -6 to 6
- history: bfloat16 [786432, 512], P('dev'), may hold values from -5 to 5
- batch_clusters: int32 [128, 48], replicated, may hold values from 0 to 6143, as said below
- pull_list: int32 [128, 128], P('dev'), may hold values from -1 to 47, as said below
- halo_ref: int32 [128, 48], P('dev'), may hold values from 0 to 127, as said below
- in_ref: int32 [128, 48], P('dev'), may hold values from 0 to 47
- tiles: bfloat16 [6144, 3, 128, 128], P('dev'), may hold values from -0.3125 to 0.3125
- w_in: bfloat16 [128, 512], replicated, may hold values from -0.5 to 0.5
- w_layers: bfloat16 [2, 512, 512], replicated, may hold values from -0.25 to 0.25
Outputs:
- second_layer: bfloat16 [786432, 512], P('dev')
- new_history: bfloat16 [786432, 512], P('dev')
The draws below stay inside these ranges and needn't reach their ends.
Inputs may be any that keep to these rules, and one draw needn't show every extreme that they name: `batch_clusters`: every cluster id appears exactly once. The ids of one device's batch owned by one owner (id // 48) number at most 1, and that many in some pairs. `pull_list`: entry o + m of a device's row is a cluster slot at owner o, or -1 for an empty slot. Some owner gets a live entry from every device. `halo_ref`: every entry points to a live entry of the same device's row of pull_list.
All inputs are finite; a program needn't handle non-finite values.
Results may differ from the reference program's by a relative error of at most 0.0052.
Values may be sent and summed in bfloat16 or wider, within the bound.
A program may use at most 256 MiB of HBM per device.

```python
import math
import jax
import jax.numpy as jnp
from jax import lax

D = 512
F = 128
BLK = 128
NB = 48
HSLOT = 128
LAYERS = 2
MOST = 1
CLUSTERS = 6144
NODES = 786432
N_DEV = 128


def halo_plan(key):
    key = jax.random.fold_in(key, 7)
    key_one, key_two, key_three, key_four = jax.random.split(key, 4)
    ranges = jax.random.randint(key_four, (N_DEV, 1), HSLOT // 4, HSLOT + 1)
    references = jax.random.randint(key_one, (N_DEV, NB), 0, ranges)
    chosen = jax.random.randint(key_two, (), 0, N_DEV)
    column = jnp.arange(NB)
    leading = chosen * MOST + column
    references = jnp.where(column[None, :] < MOST, leading[None, :], references).astype(jnp.int32)
    active = jnp.any(references[:, :, None] == jnp.arange(HSLOT)[None, None, :], axis=1)
    picked = jax.random.randint(key_three, (N_DEV, HSLOT), 0, NB)
    wanted = jnp.where(active, picked, -1).astype(jnp.int32)
    return (wanted, references)


def draw_pull_list(key, part):
    wanted, references = halo_plan(key)
    return wanted


def draw_halo_ref(key, part):
    wanted, references = halo_plan(key)
    return references


def draw_batch_clusters(key, part):
    key = jax.random.fold_in(key, 1)
    key_one, key_two, key_three = jax.random.split(key, 3)
    offsets = jax.random.permutation(key_one, N_DEV)
    ordering = jax.vmap(lambda subkey: jax.random.permutation(subkey, NB))(jax.random.split(key_two, N_DEV))
    slot_perm = jax.vmap(lambda subkey: jax.random.permutation(subkey, NB))(jax.random.split(key_three, N_DEV))
    owner_ids = (offsets[:, None] + ordering) % N_DEV
    places = slot_perm[owner_ids, ordering]
    return (owner_ids * NB + places).astype(jnp.int32)


def touch_ends(array, key, smallest, high):
    dims = array.shape
    place = [jax.random.randint(jax.random.fold_in(key, axis), (), 0, dims[axis]) for axis in range(len(dims))]
    array = array.at[tuple(place)].set(smallest)
    longest = dims.index(max(dims))
    place[longest] = (place[longest] + 1) % dims[longest]
    return array.at[tuple(place)].set(high)


def steps_of(stream_key, dims, pieces, low, top_value):
    gain = 1.0
    for position, blocks in pieces:
        draws = jax.random.uniform(jax.random.fold_in(jax.random.fold_in(stream_key, 6), position), (blocks,), jnp.float32, low / len(pieces), top_value / len(pieces))
        gain = gain * jnp.repeat(jnp.exp(draws), dims[position] // blocks).reshape((-1,) + (1,) * (len(dims) - 1 - position))
    return gain


def scatter_about(rng, extent, width, bound, shards=(), kind=jnp.bfloat16):
    values = jax.random.normal(rng, extent, jnp.float32) * width
    if len(shards) > 0:
        values = steps_of(rng, extent, shards, -0.22, 0.18) * values
    return jnp.clip(values, min=-bound, max=bound).astype(kind)


def setup_inputs(seed: int = 0) -> dict:
    seeds = jax.random.split(jax.random.key(seed), 10)
    return {
        "features": scatter_about(seeds[0], (NODES, F), 1.0, 6.0, ((0, 128),)),
        "history": scatter_about(seeds[1], (NODES, D), 0.7, 5.0, ((0, 128),)),
        "batch_clusters": draw_batch_clusters(jax.random.fold_in(seeds[9], 71), 0),
        "pull_list": draw_pull_list(jax.random.fold_in(seeds[9], 71), 0),
        "halo_ref": draw_halo_ref(jax.random.fold_in(seeds[9], 71), 0),
        "in_ref": touch_ends(jax.random.randint(seeds[5], (N_DEV, NB), 0, NB), jax.random.fold_in(seeds[5], 1), 0, NB - 1).astype(jnp.int32),
        "tiles": scatter_about(seeds[6], (CLUSTERS, 3, BLK, BLK), (3 * BLK) ** -0.5, 0.3125, ((0, 128),)),
        "w_in": scatter_about(seeds[7], (F, D), F ** -0.5, 0.5),
        "w_layers": scatter_about(seeds[8], (LAYERS, D, D), D ** -0.5, 0.25),
    }


restart = 0.1
strength = 0.5


def project(blocks_in, weight):
    flat = blocks_in.reshape(-1, blocks_in.shape[2])
    out = jax.nn.relu(jnp.dot(flat, weight, preferred_element_type=jnp.float32)).astype(jnp.bfloat16)
    return out.reshape(blocks_in.shape[0], blocks_in.shape[1], weight.shape[1])


def propagate(state, halo_state, tile_set, neighbours, initial, weight, layer):
    mix_rate = math.log(strength / layer + 1.0)
    inside = jnp.take(state, neighbours, axis=0)
    tiles32 = tile_set.astype(jnp.float32)
    aggregate = jnp.einsum('bij,bjd->bid', tiles32[:, 0], state.astype(jnp.float32))
    aggregate = aggregate + jnp.einsum('bij,bjd->bid', tiles32[:, 1], inside.astype(jnp.float32))
    aggregate = aggregate + jnp.einsum('bij,bjd->bid', tiles32[:, 2], halo_state.astype(jnp.float32))
    support = (1.0 - restart) * aggregate + restart * initial.astype(jnp.float32)
    flat = support.astype(jnp.bfloat16).reshape(-1, weight.shape[0])
    mixed = jnp.dot(flat, weight, preferred_element_type=jnp.float32).reshape(support.shape)
    return jax.nn.relu((1.0 - mix_rate) * support + mix_rate * mixed).astype(jnp.bfloat16)


def reference(features, history, batch_clusters, pull_list, halo_ref, in_ref, tiles, w_in, w_layers):
    feat_blocks = features.reshape(CLUSTERS, BLK, F)
    hist_blocks = history.reshape(CLUSTERS, BLK, D)
    slot_owner = (jnp.arange(HSLOT) // MOST).astype(jnp.int32)
    wanted = (slot_owner[None, :] * NB + jnp.maximum(pull_list, 0)).astype(jnp.int32)
    halo_cluster = jnp.take_along_axis(wanted, halo_ref, axis=1).astype(jnp.int32)
    tile_dev = tiles.reshape(N_DEV, NB, 3, BLK, BLK)

    def one_device(items):
        tile_set, clusters, halo_ids, neighbours = items
        initial = project(jnp.take(feat_blocks, clusters, axis=0), w_in)
        halo_initial = project(jnp.take(feat_blocks, halo_ids, axis=0), w_in)
        halo_hist = jnp.take(hist_blocks, halo_ids, axis=0)
        first = propagate(initial, halo_initial, tile_set, neighbours, initial, w_layers[0], 1)
        second = propagate(first, halo_hist, tile_set, neighbours, initial, w_layers[1], 2)
        return first, second

    first_layer, second_layer = lax.map(one_device, (tile_dev, batch_clusters, halo_cluster, in_ref))
    new_blocks = hist_blocks.at[batch_clusters.reshape(-1)].set(first_layer.reshape(CLUSTERS, BLK, D))
    return second_layer.reshape(NODES, D), new_blocks.reshape(NODES, D)
```

```python
import functools
import math

import jax
import jax.numpy as jnp
from jax import lax
from jax.experimental import pallas as pl
from jax.experimental.pallas import tpu as pltpu
from jax.sharding import PartitionSpec as P

restart = 0.1
strength = 0.5
lanes = 128
vmem_bytes = 56 * 1024 * 1024
bf16 = jnp.bfloat16
f32 = jnp.float32


def params():
    return pltpu.CompilerParams(vmem_limit_bytes=vmem_bytes)


def regroup_body(inner, outer, x_ref, o_ref, wide):
    chunk = 256

    def widen(i, carry):
        rows = pl.ds(pl.multiple_of(i * chunk, chunk), chunk)
        wide[rows, :] = x_ref[rows, :].astype(f32)
        return carry

    lax.fori_loop(0, inner * outer // chunk, widen, 0)

    def move(g, carry):
        rows = pl.ds(pl.multiple_of(g * inner, inner), inner)
        o_ref[rows, :] = wide[pl.ds(g, inner, stride=outer), :].astype(bf16)
        return carry

    lax.fori_loop(0, outer, move, 0, unroll=4)


def regroup(x, inner, outer, split=1, join=1):
    rows = inner * outer
    steps = max(split, join)
    return pl.pallas_call(
        functools.partial(regroup_body, inner, outer),
        grid=(steps,),
        in_specs=[pl.BlockSpec((rows, lanes), (lambda q: (0, q)) if split > 1 else (lambda q: (q, 0)))],
        out_specs=pl.BlockSpec((rows, lanes), (lambda q: (0, q)) if join > 1 else (lambda q: (q, 0))),
        out_shape=jax.ShapeDtypeStruct((rows * steps // join, lanes * join), bf16),
        scratch_shapes=[pltpu.VMEM((rows, lanes), f32)],
        compiler_params=params(),
        cost_estimate=pl.CostEstimate(flops=0, bytes_accessed=rows * steps * lanes * 24, transcendentals=0),
    )(x)


def gather_body(height, per, index, x_ref, o_ref, wide, picked):
    step = pl.program_id(0)
    chunk = 512

    @pl.when(step == 0)
    def _():
        def widen(i, carry):
            value = x_ref[pl.ds(pl.multiple_of(i * chunk, chunk), chunk), :].astype(f32)
            slots = pl.ds(pl.multiple_of(i * (chunk // height), chunk // height), chunk // height)
            wide[slots] = value.reshape(chunk // height, height, lanes) if height > 1 else value
            return carry

        lax.fori_loop(0, x_ref.shape[0] // chunk, widen, 0)

    def pick(j, carry):
        i = index[step * per + j]
        if height > 1:
            picked[j] = wide[i]
        else:
            picked[pl.ds(j, 1), :] = wide[pl.ds(i, 1), :]
        return carry

    lax.fori_loop(0, per, pick, 0, unroll=8)

    def narrow(i, carry):
        slots = pl.ds(pl.multiple_of(i * (chunk // height), chunk // height), chunk // height)
        value = picked[slots]
        value = value.reshape(chunk, lanes) if height > 1 else value
        o_ref[pl.ds(pl.multiple_of(i * chunk, chunk), chunk), :] = value.astype(bf16)
        return carry

    lax.fori_loop(0, per * height // chunk, narrow, 0)


def gather(x, index, height, steps):
    rows = x.shape[0]
    per = index.shape[0] // steps
    tail = (height, lanes) if height > 1 else (lanes,)
    return pl.pallas_call(
        functools.partial(gather_body, height, per),
        grid_spec=pltpu.PrefetchScalarGridSpec(
            num_scalar_prefetch=1,
            grid=(steps,),
            in_specs=[pl.BlockSpec((rows, lanes), lambda i, *_: (0, 0))],
            out_specs=pl.BlockSpec((per * height, lanes), lambda i, *_: (i, 0)),
            scratch_shapes=[
                pltpu.VMEM((rows // height,) + tail, f32),
                pltpu.VMEM((per,) + tail, f32),
            ],
        ),
        out_shape=jax.ShapeDtypeStruct((per * steps * height, lanes), bf16),
        compiler_params=params(),
        cost_estimate=pl.CostEstimate(flops=0, bytes_accessed=60_000_000, transcendentals=0),
    )(index, x)


def scatter_body(height, per, steps, index, x_ref, o_ref, wide, loaded):
    step = pl.program_id(0)
    chunk = 512

    def widen(i, carry):
        value = x_ref[pl.ds(pl.multiple_of(i * chunk, chunk), chunk), :].astype(f32)
        slots = pl.ds(pl.multiple_of(i * (chunk // height), chunk // height), chunk // height)
        loaded[slots] = value.reshape(chunk // height, height, lanes)
        return carry

    lax.fori_loop(0, per * height // chunk, widen, 0)

    def place(j, carry):
        wide[index[step * per + j]] = loaded[j]
        return carry

    lax.fori_loop(0, per, place, 0, unroll=8)

    @pl.when(step == steps - 1)
    def _():
        def narrow(i, carry):
            slots = pl.ds(pl.multiple_of(i * (chunk // height), chunk // height), chunk // height)
            o_ref[pl.ds(pl.multiple_of(i * chunk, chunk), chunk), :] = (
                wide[slots].reshape(chunk, lanes).astype(bf16)
            )
            return carry

        lax.fori_loop(0, o_ref.shape[0] // chunk, narrow, 0)


def scatter(x, index, height, steps):
    rows = x.shape[0]
    per = index.shape[0] // steps
    return pl.pallas_call(
        functools.partial(scatter_body, height, per, steps),
        grid_spec=pltpu.PrefetchScalarGridSpec(
            num_scalar_prefetch=1,
            grid=(steps,),
            in_specs=[pl.BlockSpec((per * height, lanes), lambda i, *_: (i, 0))],
            out_specs=pl.BlockSpec((rows, lanes), lambda i, *_: (0, 0)),
            scratch_shapes=[
                pltpu.VMEM((rows // height, height, lanes), f32),
                pltpu.VMEM((per, height, lanes), f32),
            ],
        ),
        out_shape=jax.ShapeDtypeStruct((rows, lanes), bf16),
        compiler_params=params(),
        cost_estimate=pl.CostEstimate(flops=0, bytes_accessed=60_000_000, transcendentals=0),
    )(index, x)


def project(x, weight):
    return jnp.maximum(jnp.dot(x, weight, preferred_element_type=f32), 0.0).astype(bf16)


def finish(support, weight, layer):
    mix_rate = math.log(strength / layer + 1.0)
    mixed = jnp.dot(support.astype(bf16), weight, preferred_element_type=f32)
    return jnp.maximum((1.0 - mix_rate) * support + mix_rate * mixed, 0.0).astype(bf16)


def layer_body(layer, group, neighbours, x_ref, state_ref, halo_ref, t_ref, win_ref, w_ref, o_ref, support, *made):
    step = pl.program_id(0)
    block = lanes
    if layer == 1:
        state_ref = made[0]

        @pl.when(step == 0)
        def _():
            def fill(i, carry):
                rows = pl.ds(pl.multiple_of(i * 512, 512), 512)
                state_ref[rows, :] = project(x_ref[rows, :], win_ref[...])
                return carry

            lax.fori_loop(0, state_ref.shape[0] // 512, fill, 0)

    for k in range(group):
        b = step * group + k
        own = pl.ds(pl.multiple_of(b * block, block), block)
        near = pl.ds(pl.multiple_of(neighbours[b] * block, block), block)
        here = pl.ds(k * block, block)
        if layer == 1:
            far = project(halo_ref[here, :], win_ref[...])
            initial = state_ref[own, :]
        else:
            far = halo_ref[here, :]
            initial = project(x_ref[own, :], win_ref[...])
        left = jnp.concatenate([t_ref[k, 0], t_ref[k, 1], t_ref[k, 2]], axis=1)
        right = jnp.concatenate([state_ref[own, :], state_ref[near, :], far], axis=0)
        aggregate = jnp.dot(left, right, preferred_element_type=f32)
        support[here, :] = (1.0 - restart) * aggregate + restart * initial.astype(f32)
    o_ref[...] = finish(support[...], w_ref[...], layer)


def propagate(layer, neighbours, x, state, halo, halo_offset, tiles, w_in, weight):
    count = neighbours.shape[0]
    group = 4
    width = weight.shape[0]
    span = group * lanes
    fixed = lambda *shape: pl.BlockSpec(shape, lambda i, *_: (0,) * len(shape))
    scratch = [pltpu.VMEM((span, width), f32)]
    if layer == 1:
        scratch.append(pltpu.VMEM((count * lanes, width), bf16))
    return pl.pallas_call(
        functools.partial(layer_body, layer, group),
        grid_spec=pltpu.PrefetchScalarGridSpec(
            num_scalar_prefetch=1,
            grid=(count // group,),
            in_specs=[
                fixed(count * lanes, x.shape[1]),
                fixed(*state.shape),
                pl.BlockSpec((span, halo.shape[1]), lambda i, *_: (i + halo_offset // span, 0)),
                pl.BlockSpec((group, 3, lanes, lanes), lambda i, *_: (i, 0, 0, 0)),
                fixed(*w_in.shape),
                fixed(*weight.shape),
            ],
            out_specs=pl.BlockSpec((span, width), lambda i, *_: (i, 0)),
            scratch_shapes=scratch,
        ),
        out_shape=jax.ShapeDtypeStruct((count * lanes, width), bf16),
        compiler_params=params(),
        cost_estimate=pl.CostEstimate(flops=12_000_000_000, bytes_accessed=20_000_000, transcendentals=0),
    )(neighbours, x, state, halo, tiles, w_in, weight)


def exchange(x):
    devices = lax.axis_size("dev")
    parts = x.reshape(devices, x.shape[0] // devices, x.shape[1])
    return lax.all_to_all(parts, "dev", split_axis=0, concat_axis=0, tiled=True).reshape(x.shape)


def local(features, history, batch_clusters, pull_list, halo_ref, in_ref, tiles, w_in, w_layers):
    devices = lax.axis_size("dev")
    count = tiles.shape[0]
    block = tiles.shape[2]
    columns = history.shape[1] // lanes
    height = block * columns // devices
    spread = block // height
    owner = halo_ref.reshape(count)
    slots = jnp.arange(devices, dtype=jnp.int32)
    place = jnp.sum(
        jnp.where(owner[:, None] == slots[None, :], pull_list.reshape(1, devices), 0), axis=1
    )
    pulled = lax.all_gather(owner * count + place, "dev")

    feature_slices = exchange(regroup(features, count, block))
    history_slices = exchange(regroup(history, count * height, spread, split=columns))

    wanted = jnp.concatenate([batch_clusters, pulled], axis=1).reshape(-1)
    inputs = exchange(gather(feature_slices, wanted, 1, 8))
    inputs = regroup(inputs, devices, 2 * count)

    halo_rows = exchange(gather(history_slices, pulled.reshape(-1), height, 8))

    neighbours = in_ref.reshape(count)
    first_layer = propagate(
        1, neighbours, inputs, w_in, inputs, count * block, tiles, w_in, w_layers[0]
    )
    pushed = exchange(regroup(first_layer, count * height, spread, split=columns))
    halo_history = regroup(halo_rows, spread, count * height, join=columns)
    pushed = exchange(scatter(pushed, batch_clusters.reshape(-1), height, 8))
    second_layer = propagate(
        2, neighbours, inputs, first_layer, halo_history, 0, tiles, w_in, w_layers[1]
    )
    new_history = regroup(pushed, spread, count * height, join=columns)
    return (second_layer, new_history)


def solution(mesh):
    placed = (
        P("dev", None),
        P("dev", None),
        P(),
        P("dev", None),
        P("dev", None),
        P("dev", None),
        P("dev", None, None, None),
        P(),
        P(),
    )
    return jax.shard_map(
        local,
        mesh=mesh,
        in_specs=placed,
        out_specs=(P("dev", None), P("dev", None)),
        check_vma=False,
    )
```

```python
import functools
import math

import jax
import jax.numpy as jnp
from jax import lax
from jax.experimental import pallas as pl
from jax.experimental.pallas import tpu as pltpu
from jax.sharding import PartitionSpec as P

restart = 0.1
strength = 0.5
lanes = 128
vmem_bytes = 56 * 1024 * 1024
bf16 = jnp.bfloat16
f32 = jnp.float32


def params():
    return pltpu.CompilerParams(vmem_limit_bytes=vmem_bytes)


def regroup_body(inner, outer, x_ref, o_ref, wide):
    chunk = 256

    def widen(i, carry):
        rows = pl.ds(pl.multiple_of(i * chunk, chunk), chunk)
        wide[rows, :] = x_ref[rows, :].astype(f32)
        return carry

    lax.fori_loop(0, inner * outer // chunk, widen, 0)

    def move(g, carry):
        rows = pl.ds(pl.multiple_of(g * inner, inner), inner)
        o_ref[rows, :] = wide[pl.ds(g, inner, stride=outer), :].astype(bf16)
        return carry

    lax.fori_loop(0, outer, move, 0, unroll=4)


def regroup(x, inner, outer, split=1, join=1):
    rows = inner * outer
    steps = max(split, join)
    return pl.pallas_call(
        functools.partial(regroup_body, inner, outer),
        grid=(steps,),
        in_specs=[pl.BlockSpec((rows, lanes), (lambda q: (0, q)) if split > 1 else (lambda q: (q, 0)))],
        out_specs=pl.BlockSpec((rows, lanes), (lambda q: (0, q)) if join > 1 else (lambda q: (q, 0))),
        out_shape=jax.ShapeDtypeStruct((rows * steps // join, lanes * join), bf16),
        scratch_shapes=[pltpu.VMEM((rows, lanes), f32)],
        compiler_params=params(),
        cost_estimate=pl.CostEstimate(flops=0, bytes_accessed=rows * steps * lanes * 24, transcendentals=0),
    )(x)


def gather_body(height, per, index, x_ref, o_ref, wide, picked):
    step = pl.program_id(0)
    chunk = 512

    @pl.when(step == 0)
    def _():
        def widen(i, carry):
            value = x_ref[pl.ds(pl.multiple_of(i * chunk, chunk), chunk), :].astype(f32)
            slots = pl.ds(pl.multiple_of(i * (chunk // height), chunk // height), chunk // height)
            wide[slots] = value.reshape(chunk // height, height, lanes) if height > 1 else value
            return carry

        lax.fori_loop(0, x_ref.shape[0] // chunk, widen, 0)

    def pick(j, carry):
        i = index[step * per + j]
        if height > 1:
            picked[j] = wide[i]
        else:
            picked[pl.ds(j, 1), :] = wide[pl.ds(i, 1), :]
        return carry

    lax.fori_loop(0, per, pick, 0, unroll=8)

    def narrow(i, carry):
        slots = pl.ds(pl.multiple_of(i * (chunk // height), chunk // height), chunk // height)
        value = picked[slots]
        value = value.reshape(chunk, lanes) if height > 1 else value
        o_ref[pl.ds(pl.multiple_of(i * chunk, chunk), chunk), :] = value.astype(bf16)
        return carry

    lax.fori_loop(0, per * height // chunk, narrow, 0)


def gather(x, index, height, steps):
    rows = x.shape[0]
    per = index.shape[0] // steps
    tail = (height, lanes) if height > 1 else (lanes,)
    return pl.pallas_call(
        functools.partial(gather_body, height, per),
        grid_spec=pltpu.PrefetchScalarGridSpec(
            num_scalar_prefetch=1,
            grid=(steps,),
            in_specs=[pl.BlockSpec((rows, lanes), lambda i, *_: (0, 0))],
            out_specs=pl.BlockSpec((per * height, lanes), lambda i, *_: (i, 0)),
            scratch_shapes=[
                pltpu.VMEM((rows // height,) + tail, f32),
                pltpu.VMEM((per,) + tail, f32),
            ],
        ),
        out_shape=jax.ShapeDtypeStruct((per * steps * height, lanes), bf16),
        compiler_params=params(),
        cost_estimate=pl.CostEstimate(flops=0, bytes_accessed=60_000_000, transcendentals=0),
    )(index, x)


def scatter_body(height, per, steps, index, x_ref, o_ref, wide, loaded):
    step = pl.program_id(0)
    chunk = 512

    def widen(i, carry):
        value = x_ref[pl.ds(pl.multiple_of(i * chunk, chunk), chunk), :].astype(f32)
        slots = pl.ds(pl.multiple_of(i * (chunk // height), chunk // height), chunk // height)
        loaded[slots] = value.reshape(chunk // height, height, lanes)
        return carry

    lax.fori_loop(0, per * height // chunk, widen, 0)

    def place(j, carry):
        wide[index[step * per + j]] = loaded[j]
        return carry

    lax.fori_loop(0, per, place, 0, unroll=8)

    @pl.when(step == steps - 1)
    def _():
        def narrow(i, carry):
            slots = pl.ds(pl.multiple_of(i * (chunk // height), chunk // height), chunk // height)
            o_ref[pl.ds(pl.multiple_of(i * chunk, chunk), chunk), :] = (
                wide[slots].reshape(chunk, lanes).astype(bf16)
            )
            return carry

        lax.fori_loop(0, o_ref.shape[0] // chunk, narrow, 0)


def scatter(x, index, height, steps):
    rows = x.shape[0]
    per = index.shape[0] // steps
    return pl.pallas_call(
        functools.partial(scatter_body, height, per, steps),
        grid_spec=pltpu.PrefetchScalarGridSpec(
            num_scalar_prefetch=1,
            grid=(steps,),
            in_specs=[pl.BlockSpec((per * height, lanes), lambda i, *_: (i, 0))],
            out_specs=pl.BlockSpec((rows, lanes), lambda i, *_: (0, 0)),
            scratch_shapes=[
                pltpu.VMEM((rows // height, height, lanes), f32),
                pltpu.VMEM((per, height, lanes), f32),
            ],
        ),
        out_shape=jax.ShapeDtypeStruct((rows, lanes), bf16),
        compiler_params=params(),
        cost_estimate=pl.CostEstimate(flops=0, bytes_accessed=60_000_000, transcendentals=0),
    )(index, x)


def project(x, weight):
    return jnp.maximum(jnp.dot(x, weight, preferred_element_type=f32), 0.0).astype(bf16)


def finish(support, weight, layer):
    mix_rate = math.log(strength / layer + 1.0)
    mixed = jnp.dot(support.astype(bf16), weight, preferred_element_type=f32)
    return jnp.maximum((1.0 - mix_rate) * support + mix_rate * mixed, 0.0).astype(bf16)


def layer_body(layer, group, neighbours, x_ref, state_ref, halo_ref, t_ref, win_ref, w_ref, o_ref, support, *made):
    step = pl.program_id(0)
    block = lanes
    if layer == 1:
        state_ref = made[0]

        @pl.when(step == 0)
        def _():
            def fill(i, carry):
                rows = pl.ds(pl.multiple_of(i * 512, 512), 512)
                state_ref[rows, :] = project(x_ref[rows, :], win_ref[...])
                return carry

            lax.fori_loop(0, state_ref.shape[0] // 512, fill, 0)

    for k in range(group):
        b = step * group + k
        own = pl.ds(pl.multiple_of(b * block, block), block)
        near = pl.ds(pl.multiple_of(neighbours[b] * block, block), block)
        here = pl.ds(k * block, block)
        if layer == 1:
            far = project(halo_ref[here, :], win_ref[...])
            initial = state_ref[own, :]
        else:
            far = halo_ref[here, :]
            initial = project(x_ref[own, :], win_ref[...])
        left = jnp.concatenate([t_ref[k, 0], t_ref[k, 1], t_ref[k, 2]], axis=1)
        right = jnp.concatenate([state_ref[own, :], state_ref[near, :], far], axis=0)
        aggregate = jnp.dot(left, right, preferred_element_type=f32)
        support[here, :] = (1.0 - restart) * aggregate + restart * initial.astype(f32)
    o_ref[...] = finish(support[...], w_ref[...], layer)


def propagate(layer, neighbours, x, state, halo, halo_offset, tiles, w_in, weight):
    count = neighbours.shape[0]
    group = 4
    width = weight.shape[0]
    span = group * lanes
    fixed = lambda *shape: pl.BlockSpec(shape, lambda i, *_: (0,) * len(shape))
    scratch = [pltpu.VMEM((span, width), f32)]
    if layer == 1:
        scratch.append(pltpu.VMEM((count * lanes, width), bf16))
    return pl.pallas_call(
        functools.partial(layer_body, layer, group),
        grid_spec=pltpu.PrefetchScalarGridSpec(
            num_scalar_prefetch=1,
            grid=(count // group,),
            in_specs=[
                fixed(count * lanes, x.shape[1]),
                fixed(*state.shape),
                pl.BlockSpec((span, halo.shape[1]), lambda i, *_: (i + halo_offset // span, 0)),
                pl.BlockSpec((group, 3, lanes, lanes), lambda i, *_: (i, 0, 0, 0)),
                fixed(*w_in.shape),
                fixed(*weight.shape),
            ],
            out_specs=pl.BlockSpec((span, width), lambda i, *_: (i, 0)),
            scratch_shapes=scratch,
        ),
        out_shape=jax.ShapeDtypeStruct((count * lanes, width), bf16),
        compiler_params=params(),
        cost_estimate=pl.CostEstimate(flops=12_000_000_000, bytes_accessed=20_000_000, transcendentals=0),
    )(neighbours, x, state, halo, tiles, w_in, weight)


def exchange(x):
    devices = lax.axis_size("dev")
    parts = x.reshape(devices, x.shape[0] // devices, x.shape[1])
    return lax.all_to_all(parts, "dev", split_axis=0, concat_axis=0, tiled=True).reshape(x.shape)

MESH = pl.DeviceIdType.MESH
IDS, FEAT_OUT, HIST_OUT, FEAT_IN = range(4)


def partner(me, k):
    z, x, y, core = me // 32, me // 8 % 4, me // 2 % 4, me % 2
    return (
        (z + k // 32) % 4 * 32 + (x + k // 8 % 4) % 4 * 8 + (y + k // 2 % 4) % 4 * 2 + (core + k % 2) % 2
    )


def order(me, i):
    return partner(me, i * (37 + 54 * (me % 2)) % 128)


def wait_all(ref, rows, sem):
    part = ref.at[pl.ds(0, rows)]
    pltpu.make_async_copy(part, part, sem).wait()


def send(src, dst, sems, way, peer):
    pltpu.make_async_remote_copy(
        src_ref=src,
        dst_ref=dst,
        send_sem=sems.at[0, way],
        recv_sem=sems.at[1, way],
        device_id=(peer,),
        device_id_type=MESH,
    ).start()


def widen(src, dst, offset, rows):
    chunk = 256

    def step(i, carry):
        at = pl.multiple_of(i * chunk, chunk)
        dst[pl.ds(offset + at, chunk), :] = src[pl.ds(at, chunk), :].astype(f32)
        return carry

    lax.fori_loop(0, rows // chunk, step, 0)


def front_body(
    batch, ids_ref, feat_ref, hist_ref,
    inputs, hist_mid, ids_out,
    ids_mid, ids_smem, feat_wide, wide, stage, feat_send, feat_mid, inputs_send, hist_send, picked,
    sems, local_sem, stage_sem,
):
    devices = 128
    count = 48
    me = lax.axis_index("dev")
    rows = count * lanes

    def load_history(q):
        return pltpu.make_async_copy(
            hist_ref.at[:, pl.ds(q * lanes, lanes)], stage.at[q % 2], stage_sem.at[q % 2]
        )

    load_history(0).start()
    load_history(1).start()
    barrier = pltpu.get_barrier_semaphore()

    def greet(i, carry):
        pl.semaphore_signal(barrier, inc=1, device_id=(partner(me, i),), device_id_type=MESH)
        return carry

    lax.fori_loop(1, devices, greet, 0)
    pl.semaphore_wait(barrier, devices - 1)

    def send_ids(i, carry):
        send(ids_ref, ids_mid.at[me], sems, IDS, order(me, i))
        return carry

    lax.fori_loop(1, devices, send_ids, 0)
    pltpu.make_async_copy(ids_ref, ids_mid.at[me], local_sem.at[IDS]).start()

    widen(feat_ref, feat_wide, 0, rows)

    def at(ref, slot, size):
        return ref.at[pl.ds(pl.multiple_of(slot * size, size), size)]

    def pack_feat(m):
        feat_send[pl.ds(pl.multiple_of(m * count, count), count), :] = feat_wide[
            pl.ds(m, count, stride=lanes), :
        ].astype(bf16)

    def spread_feat(i, carry):
        m = order(me, i)
        pack_feat(m)
        send(at(feat_send, m, count), at(feat_mid, me, count), sems, FEAT_OUT, m)
        return carry

    lax.fori_loop(1, devices, spread_feat, 0)
    pack_feat(me)
    pltpu.make_async_copy(at(feat_send, me, count), at(feat_mid, me, count), local_sem.at[FEAT_OUT]).start()

    for q in range(4):
        load_history(q).wait()
        widen(stage.at[q % 2], wide, q * rows, rows)
        if q + 2 < 4:
            load_history(q + 2).start()

    height = 4 * count

    def pack_hist(m):
        first = m // 32 * rows + m % 32
        hist_send[pl.ds(pl.multiple_of(m * height, height), height), :] = wide[
            pl.ds(first, height, stride=32), :
        ].astype(bf16)

    def spread_hist(i, carry):
        m = order(me, i)
        pack_hist(m)
        for piece in range(3):
            src = hist_send.at[pl.ds(pl.multiple_of(m * height + piece * 64, 64), 64)]
            dst = hist_mid.at[pl.ds(pl.multiple_of(me * height + piece * 64, 64), 64)]
            send(src, dst, sems, HIST_OUT, m)
        return carry

    pack_hist(me)
    pltpu.make_async_copy(at(hist_send, me, height), at(hist_mid, me, height), local_sem.at[HIST_OUT]).start()
    lax.fori_loop(1, devices // 2, spread_hist, 0)

    pltpu.make_async_copy(ids_ref, ids_mid.at[me], local_sem.at[IDS]).wait()
    wait_all(ids_mid, devices - 1, sems.at[1, IDS])
    to_smem = pltpu.make_async_copy(ids_mid, ids_smem, local_sem.at[FEAT_IN])
    to_smem.start()
    to_smem.wait()
    ids_copy = pltpu.make_async_copy(ids_mid, ids_out, local_sem.at[FEAT_IN])
    ids_copy.start()
    ids_copy.wait()
    pltpu.make_async_copy(at(feat_send, me, count), at(feat_mid, me, count), local_sem.at[FEAT_OUT]).wait()
    wait_all(feat_mid, (devices - 1) * count, sems.at[1, FEAT_OUT])
    widen(feat_mid, feat_wide, 0, rows)
    both = 2 * count

    def pick_feat(d):
        for b in range(count):
            picked[pl.ds(b, 1), :] = feat_wide[pl.ds(batch[d, b], 1), :]
        for b in range(count):
            picked[pl.ds(count + b, 1), :] = feat_wide[pl.ds(ids_smem[d, 0, b], 1), :]
        inputs_send[pl.ds(pl.multiple_of(d * both, both), both), :] = picked[pl.ds(0, both), :].astype(bf16)

    def serve_feat(i, carry):
        d = order(me, i)
        pick_feat(d)
        send(at(inputs_send, d, both), at(inputs, me, both), sems, FEAT_IN, d)
        return carry

    lax.fori_loop(1, devices, serve_feat, 0)
    pick_feat(me)
    pltpu.make_async_copy(at(inputs_send, me, both), at(inputs, me, both), local_sem.at[FEAT_IN]).start()
    lax.fori_loop(devices // 2, devices, spread_hist, 0)
    pltpu.make_async_copy(at(inputs_send, me, both), at(inputs, me, both), local_sem.at[FEAT_IN]).wait()
    wait_all(inputs, (devices - 1) * both, sems.at[1, FEAT_IN])
    pltpu.make_async_copy(at(hist_send, me, height), at(hist_mid, me, height), local_sem.at[HIST_OUT]).wait()
    wait_all(hist_mid, (devices - 1) * height, sems.at[1, HIST_OUT])
    wait_all(ids_mid, devices - 1, sems.at[0, IDS])
    wait_all(feat_mid, (devices - 1) * count, sems.at[0, FEAT_OUT])
    wait_all(inputs, (devices - 1) * both, sems.at[0, FEAT_IN])
    wait_all(hist_mid, (devices - 1) * height, sems.at[0, HIST_OUT])


def front(batch, ids, features, history):
    devices, count = batch.shape
    rows = features.shape[0]
    anywhere = pl.BlockSpec(memory_space=pl.ANY)
    smem = pl.BlockSpec(memory_space=pltpu.SMEM)
    vmem = pl.BlockSpec(memory_space=pltpu.VMEM)
    return pl.pallas_call(
        front_body,
        in_specs=[smem, vmem, vmem, anywhere],
        out_specs=[anywhere, anywhere, anywhere],
        out_shape=[
            jax.ShapeDtypeStruct((2 * rows, lanes), bf16),
            jax.ShapeDtypeStruct((4 * rows, lanes), bf16),
            jax.ShapeDtypeStruct((devices, 1, lanes), jnp.int32),
        ],
        scratch_shapes=[
            pltpu.VMEM((devices, 1, lanes), jnp.int32),
            pltpu.SMEM((devices, 1, lanes), jnp.int32),
            pltpu.VMEM((rows, lanes), f32),
            pltpu.VMEM((4 * rows, lanes), f32),
            pltpu.VMEM((2, rows, lanes), bf16),
            pltpu.VMEM((rows, lanes), bf16),
            pltpu.VMEM((rows, lanes), bf16),
            pltpu.VMEM((2 * rows, lanes), bf16),
            pltpu.VMEM((4 * rows, lanes), bf16),
            pltpu.VMEM((4 * count, lanes), f32),
            pltpu.SemaphoreType.DMA((2, 4)),
            pltpu.SemaphoreType.DMA((4,)),
            pltpu.SemaphoreType.DMA((2,)),
        ],
        compiler_params=pltpu.CompilerParams(
            vmem_limit_bytes=vmem_bytes, collective_id=1, has_side_effects=True
        ),
        cost_estimate=pl.CostEstimate(flops=0, bytes_accessed=60_000_000, transcendentals=0),
    )(batch, ids, features, history)


def local(features, history, batch_clusters, pull_list, halo_ref, in_ref, tiles, w_in, w_layers):
    devices = lax.axis_size("dev")
    count = tiles.shape[0]
    block = tiles.shape[2]
    columns = history.shape[1] // lanes
    height = block * columns // devices
    spread = block // height
    owner = halo_ref.reshape(count)
    slots = jnp.arange(devices, dtype=jnp.int32)
    place = jnp.sum(
        jnp.where(owner[:, None] == slots[None, :], pull_list.reshape(1, devices), 0), axis=1
    )
    mine = jnp.pad(owner * count + place, (0, lanes - count)).reshape(1, lanes)
    inputs, history_slices, pulled = front(batch_clusters, mine, features, history)
    inputs = regroup(inputs, devices, 2 * count)
    pulled = pulled[:, 0, :count]

    halo_rows = exchange(gather(history_slices, pulled.reshape(-1), height, 8))

    neighbours = in_ref.reshape(count)
    first_layer = propagate(
        1, neighbours, inputs, w_in, inputs, count * block, tiles, w_in, w_layers[0]
    )
    pushed = exchange(regroup(first_layer, count * height, spread, split=columns))
    halo_history = regroup(halo_rows, spread, count * height, join=columns)
    pushed = exchange(scatter(pushed, batch_clusters.reshape(-1), height, 8))
    second_layer = propagate(
        2, neighbours, inputs, first_layer, halo_history, 0, tiles, w_in, w_layers[1]
    )
    new_history = regroup(pushed, spread, count * height, join=columns)
    return (second_layer, new_history)


def solution(mesh):
    placed = (
        P("dev", None),
        P("dev", None),
        P(),
        P("dev", None),
        P("dev", None),
        P("dev", None),
        P("dev", None, None, None),
        P(),
        P(),
    )
    return jax.shard_map(
        local,
        mesh=mesh,
        in_specs=placed,
        out_specs=(P("dev", None), P("dev", None)),
        check_vma=False,
    )
```

```python
import functools
import math

import jax
import jax.numpy as jnp
from jax import lax
from jax.experimental import pallas as pl
from jax.experimental.pallas import tpu as pltpu
from jax.sharding import PartitionSpec as P

restart = 0.1
strength = 0.5
lanes = 128
devices = 128
count = 48
rows = count * lanes
height = 4 * count
both = 2 * count
group = 4
span = group * lanes
piece = 64
vmem_bytes = 60 * 1024 * 1024
bf16 = jnp.bfloat16
f32 = jnp.float32
MESH = pl.DeviceIdType.MESH
IDS, FEAT_OUT, HIST_OUT, FEAT_IN, PUSH_OUT, HIST_IN, PUSH_IN = range(7)
WAYS = 7


def partner(me, k):
    z, x, y, core = me // 32, me // 8 % 4, me // 2 % 4, me % 2
    return (
        (z + k // 32) % 4 * 32 + (x + k // 8 % 4) % 4 * 8 + (y + k // 2 % 4) % 4 * 2 + (core + k % 2) % 2
    )


def order(me, i):
    return partner(me, i * (37 + 54 * (me % 2)) % devices)


def at(ref, slot, size):
    return ref.at[pl.ds(pl.multiple_of(slot * size, size), size)]


def wait_all(ref, size, sem):
    part = ref.at[pl.ds(0, size)]
    pltpu.make_async_copy(part, part, sem).wait()


def send(src, dst, sems, way, peer):
    pltpu.make_async_remote_copy(
        src_ref=src,
        dst_ref=dst,
        send_sem=sems.at[0, way],
        recv_sem=sems.at[1, way],
        device_id=(peer,),
        device_id_type=MESH,
    ).start()


def send_pieces(src_ref, src_slot, dst_ref, dst_slot, sems, way, peer):
    for part in range(height // piece):
        src = src_ref.at[pl.ds(pl.multiple_of(src_slot * height + part * piece, piece), piece)]
        dst = dst_ref.at[pl.ds(pl.multiple_of(dst_slot * height + part * piece, piece), piece)]
        send(src, dst, sems, way, peer)


def widen(src, dst, offset, size):
    chunk = 256

    def step(i, carry):
        here = pl.multiple_of(i * chunk, chunk)
        dst[pl.ds(offset + here, chunk), :] = src[pl.ds(here, chunk), :].astype(f32)
        return carry

    lax.fori_loop(0, size // chunk, step, 0)


def project(x, weight):
    return jnp.maximum(jnp.dot(x, weight, preferred_element_type=f32), 0.0).astype(bf16)


def mix(left, right, initial):
    aggregate = jnp.dot(left, right, preferred_element_type=f32)
    return (1.0 - restart) * aggregate + restart * initial.astype(f32)


def finish(support, weight, layer):
    mix_rate = math.log(strength / layer + 1.0)
    mixed = jnp.dot(support.astype(bf16), weight, preferred_element_type=f32)
    return jnp.maximum((1.0 - mix_rate) * support + mix_rate * mixed, 0.0).astype(bf16)


def step_body(
    batch, inverse, near, ids_ref, feat_ref, hist_ref, tile_ref, win_ref, w_ref,
    second, inputs, hist_mid, halo, push_mid, pushed,
    ids_mid, ids_smem, feat_wide, wide, stage, feat_send, feat_mid, inputs_send, given,
    wide_send, halo_send, state, support, tiles, ready, picked,
    sems, local_sem, stage_sem, tile_sem, out_sem,
):
    me = lax.axis_index("dev")

    def load_history(q):
        return pltpu.make_async_copy(
            hist_ref.at[:, pl.ds(q * lanes, lanes)], stage.at[q % 2], stage_sem.at[q % 2]
        )

    def load_part(src, q):
        return pltpu.make_async_copy(src.at[pl.ds(q * rows, rows)], stage.at[q % 2], stage_sem.at[q % 2])

    def load_wide(load, parts):
        for q in range(parts):
            load(q).wait()
            widen(stage.at[q % 2], wide, q * rows, rows)
            if q + 2 < parts:
                load(q + 2).start()

    def keep(src, src_slot, dst, dst_slot, size, way):
        return pltpu.make_async_copy(at(src, src_slot, size), at(dst, dst_slot, size), local_sem.at[way])

    def each(body, first, last):
        def step(i, carry):
            body(order(me, i))
            return carry

        lax.fori_loop(first, last, step, 0)

    load_tiles = pltpu.make_async_copy(tile_ref, tiles, tile_sem.at[0])
    load_history(0).start()
    load_history(1).start()
    barrier = pltpu.get_barrier_semaphore()

    def greet(i, carry):
        pl.semaphore_signal(barrier, inc=1, device_id=(partner(me, i),), device_id_type=MESH)
        return carry

    lax.fori_loop(1, devices, greet, 0)
    pl.semaphore_wait(barrier, devices - 1)

    each(lambda m: send(ids_ref, ids_mid.at[me], sems, IDS, m), 1, devices)
    keep_ids = pltpu.make_async_copy(ids_ref, ids_mid.at[me], local_sem.at[IDS])
    keep_ids.start()

    widen(feat_ref, feat_wide, 0, rows)

    def pack_feat(m):
        feat_send[pl.ds(pl.multiple_of(m * count, count), count), :] = feat_wide[
            pl.ds(m, count, stride=lanes), :
        ].astype(bf16)

    def spread_feat(m):
        pack_feat(m)
        send(at(feat_send, m, count), at(feat_mid, me, count), sems, FEAT_OUT, m)

    each(spread_feat, 1, devices)
    pack_feat(me)
    keep_feat = keep(feat_send, me, feat_mid, me, count, FEAT_OUT)
    keep_feat.start()

    def pack_wide(m):
        wide_send[pl.ds(pl.multiple_of(m * height, height), height), :] = wide[
            pl.ds(m // 32 * rows + m % 32, height, stride=32), :
        ].astype(bf16)

    def spread_hist(m):
        pack_wide(m)
        send_pieces(wide_send, m, hist_mid, me, sems, HIST_OUT, m)

    load_wide(load_history, 4)
    load_tiles.start()
    pack_wide(me)
    keep_hist = keep(wide_send, me, hist_mid, me, height, HIST_OUT)
    keep_hist.start()
    each(spread_hist, 1, devices // 2)

    keep_ids.wait()
    wait_all(ids_mid, devices - 1, sems.at[1, IDS])
    to_smem = pltpu.make_async_copy(ids_mid, ids_smem, local_sem.at[IDS])
    to_smem.start()
    to_smem.wait()
    keep_feat.wait()
    wait_all(feat_mid, (devices - 1) * count, sems.at[1, FEAT_OUT])

    widen(feat_mid, feat_wide, 0, rows)

    def pick_feat(d):
        for b in range(count):
            picked[pl.ds(b, 1), :] = feat_wide[pl.ds(batch[d, b], 1), :]
        for b in range(count):
            picked[pl.ds(count + b, 1), :] = feat_wide[pl.ds(ids_smem[d, 0, b], 1), :]
        inputs_send[pl.ds(pl.multiple_of(d * both, both), both), :] = picked[pl.ds(0, both), :].astype(bf16)

    def serve_feat(d):
        pick_feat(d)
        send(at(inputs_send, d, both), at(inputs, me, both), sems, FEAT_IN, d)

    each(serve_feat, 1, devices)
    pick_feat(me)
    keep_inputs = keep(inputs_send, me, inputs, me, both, FEAT_IN)
    keep_inputs.start()
    each(spread_hist, devices // 2, devices)

    keep_inputs.wait()
    wait_all(inputs, (devices - 1) * both, sems.at[1, FEAT_IN])
    load_inputs = functools.partial(load_part, inputs)
    load_inputs(0).start()
    load_inputs(1).start()
    load_wide(load_inputs, 2)

    def order_inputs(b, carry):
        given[b] = wide[pl.ds(b, lanes, stride=both), :].astype(bf16)
        return carry

    lax.fori_loop(0, both, order_inputs, 0, unroll=2)
    load_tiles.wait()

    def tile_row(b):
        return jnp.concatenate([tiles[b, 0], tiles[b, 1], tiles[b, 2]], axis=1)

    def first_group(g, carry):
        for k in range(group):
            b = g * group + k
            states = project(
                jnp.concatenate([given[b], given[near[0, b]], given[count + b]], axis=0),
                win_ref[...],
            )
            support[pl.ds(k * lanes, lanes), :] = mix(tile_row(b), states, states[:lanes])
        made = finish(support[...], w_ref[0], 1)
        for k in range(group):
            state[g * group + k] = made[k * lanes : (k + 1) * lanes]
        for q in range(4):
            wide[pl.ds(pl.multiple_of(q * rows + g * span, span), span), :] = made[
                :, q * lanes : (q + 1) * lanes
            ].astype(f32)
        return carry

    lax.fori_loop(0, count // group, first_group, 0)

    keep_hist.wait()
    wait_all(hist_mid, (devices - 1) * height, sems.at[0, HIST_OUT])

    def spread_push(m):
        pack_wide(m)
        send_pieces(wide_send, m, push_mid, me, sems, PUSH_OUT, m)

    each(spread_push, 1, devices)
    pack_wide(me)
    keep_push = keep(wide_send, me, push_mid, me, height, PUSH_OUT)
    keep_push.start()

    wait_all(hist_mid, (devices - 1) * height, sems.at[1, HIST_OUT])
    load_mid = functools.partial(load_part, hist_mid)
    load_mid(0).start()
    load_mid(1).start()
    load_wide(load_mid, 4)

    def pick_wide(dst, d, index):
        for b in range(count):
            picked[pl.ds(4 * b, 4), :] = wide[pl.ds(index(b), 4), :]
        dst[pl.ds(pl.multiple_of(d * height, height), height), :] = picked[...].astype(bf16)

    def pick_halo(d):
        pick_wide(halo_send, d, lambda b: ids_smem[d, 0, lanes // 2 + b])

    def serve_halo(d):
        pick_halo(d)
        send_pieces(halo_send, d, halo, me, sems, HIST_IN, d)

    each(serve_halo, 1, devices)
    pick_halo(me)
    keep_halo = keep(halo_send, me, halo, me, height, HIST_IN)
    keep_halo.start()

    keep_push.wait()
    wait_all(push_mid, (devices - 1) * height, sems.at[1, PUSH_OUT])
    load_push = functools.partial(load_part, push_mid)
    load_push(0).start()
    load_push(1).start()
    wait_all(push_mid, (devices - 1) * height, sems.at[0, PUSH_OUT])
    load_wide(load_push, 4)

    def pick_push(o):
        pick_wide(wide_send, o, lambda p: inverse[o, p])

    def serve_push(o):
        pick_push(o)
        send_pieces(wide_send, o, pushed, me, sems, PUSH_IN, o)

    each(serve_push, 1, devices)
    pick_push(me)
    keep_pushed = keep(wide_send, me, pushed, me, height, PUSH_IN)
    keep_pushed.start()

    keep_halo.wait()
    wait_all(halo, (devices - 1) * height, sems.at[1, HIST_IN])
    load_halo = functools.partial(load_part, halo)
    load_halo(0).start()
    load_halo(1).start()
    load_wide(load_halo, 4)

    def halo_block(b):
        return jnp.concatenate(
            [
                jnp.concatenate(
                    [wide[pl.ds(q * rows + 4 * b + i, 32, stride=height), :] for i in range(4)], axis=0
                )
                for q in range(4)
            ],
            axis=1,
        ).astype(bf16)

    def write(g, slot):
        return pltpu.make_async_copy(
            ready.at[slot], second.at[pl.ds(pl.multiple_of(g * span, span), span)], out_sem.at[slot]
        )

    def second_pair(pair, carry):
        for slot in range(2):
            g = pair * 2 + slot
            for k in range(group):
                b = g * group + k
                initial = project(given[b], win_ref[...])
                states = jnp.concatenate([state[b], state[near[0, b]], halo_block(b)], axis=0)
                support[pl.ds(k * lanes, lanes), :] = mix(tile_row(b), states, initial)
            made = finish(support[...], w_ref[1], 2)

            @pl.when(pair > 0)
            def _():
                write(g - 2, slot).wait()

            ready[slot] = made
            write(g, slot).start()
        return carry

    lax.fori_loop(0, count // group // 2, second_pair, 0)
    for slot in range(2):
        write(count // group - 2 + slot, slot).wait()

    keep_pushed.wait()
    wait_all(pushed, (devices - 1) * height, sems.at[1, PUSH_IN])
    wait_all(ids_mid, devices - 1, sems.at[0, IDS])
    wait_all(feat_mid, (devices - 1) * count, sems.at[0, FEAT_OUT])
    wait_all(inputs, (devices - 1) * both, sems.at[0, FEAT_IN])
    wait_all(halo, (devices - 1) * height, sems.at[0, HIST_IN])
    wait_all(pushed, (devices - 1) * height, sems.at[0, PUSH_IN])


def run_step(batch, inverse, near, ids, features, history, tiles, w_in, w_layers):
    anywhere = pl.BlockSpec(memory_space=pl.ANY)
    smem = pl.BlockSpec(memory_space=pltpu.SMEM)
    vmem = pl.BlockSpec(memory_space=pltpu.VMEM)
    shape = lambda *dims: jax.ShapeDtypeStruct(dims, bf16)
    sliced = shape(4 * rows, lanes)
    return pl.pallas_call(
        step_body,
        in_specs=[smem, smem, smem, vmem, vmem, anywhere, anywhere, vmem, vmem],
        out_specs=[anywhere] * 6,
        out_shape=[shape(rows, 4 * lanes), shape(2 * rows, lanes), sliced, sliced, sliced, sliced],
        scratch_shapes=[
            pltpu.VMEM((devices, 1, lanes), jnp.int32),
            pltpu.SMEM((devices, 1, lanes), jnp.int32),
            pltpu.VMEM((rows, lanes), f32),
            pltpu.VMEM((4 * rows, lanes), f32),
            pltpu.VMEM((2, rows, lanes), bf16),
            pltpu.VMEM((rows, lanes), bf16),
            pltpu.VMEM((rows, lanes), bf16),
            pltpu.VMEM((2 * rows, lanes), bf16),
            pltpu.VMEM((both, lanes, lanes), bf16),
            pltpu.VMEM((4 * rows, lanes), bf16),
            pltpu.VMEM((4 * rows, lanes), bf16),
            pltpu.VMEM((count, lanes, 4 * lanes), bf16),
            pltpu.VMEM((span, 4 * lanes), f32),
            pltpu.VMEM((count, 3, lanes, lanes), bf16),
            pltpu.VMEM((2, span, 4 * lanes), bf16),
            pltpu.VMEM((height, lanes), f32),
            pltpu.SemaphoreType.DMA((2, WAYS)),
            pltpu.SemaphoreType.DMA((WAYS,)),
            pltpu.SemaphoreType.DMA((2,)),
            pltpu.SemaphoreType.DMA((1,)),
            pltpu.SemaphoreType.DMA((2,)),
        ],
        compiler_params=pltpu.CompilerParams(
            vmem_limit_bytes=vmem_bytes, collective_id=1, has_side_effects=True
        ),
        cost_estimate=pl.CostEstimate(flops=14_000_000_000, bytes_accessed=100_000_000, transcendentals=0),
    )(batch, inverse, near, ids, features, history, tiles, w_in, w_layers)


def place_body(pushed, second, fresh, result, wide):
    result[...] = second[...]
    widen(pushed, wide, 0, rows)

    def move(a, carry):
        fresh[pl.ds(pl.multiple_of(a * 32, 32), 32), :] = wide[pl.ds(a, 32, stride=height), :].astype(bf16)
        return carry

    lax.fori_loop(0, height, move, 0, unroll=4)


def place(pushed, second):
    full = jax.ShapeDtypeStruct((rows, 4 * lanes), bf16)
    quarter = pl.BlockSpec((rows // 4, 4 * lanes), lambda q: (q, 0))
    return pl.pallas_call(
        place_body,
        grid=(4,),
        in_specs=[pl.BlockSpec((rows, lanes), lambda q: (q, 0)), quarter],
        out_specs=[pl.BlockSpec((rows, lanes), lambda q: (0, q)), quarter],
        out_shape=[full, full],
        scratch_shapes=[pltpu.VMEM((rows, lanes), f32)],
        compiler_params=pltpu.CompilerParams(vmem_limit_bytes=vmem_bytes),
        cost_estimate=pl.CostEstimate(flops=0, bytes_accessed=40_000_000, transcendentals=0),
    )(pushed, second)


def invert(batch):
    flat = batch.reshape(-1)
    spot = jnp.arange(flat.shape[0], dtype=jnp.int32)
    owner = (flat // count)[:, None] == jnp.arange(devices, dtype=jnp.int32)[None, :]
    place = (flat % count)[:, None] == jnp.arange(count, dtype=jnp.int32)[None, :]
    low = jnp.where(place, (spot % 64)[:, None], 0).astype(bf16)
    high = jnp.where(place, (spot // 64)[:, None], 0).astype(bf16)
    found = lax.dot_general(
        owner.astype(bf16),
        jnp.concatenate([low, high], axis=1),
        (((0,), (0,)), ((), ())),
        preferred_element_type=f32,
    ).astype(jnp.int32)
    return found[:, :count] + 64 * found[:, count:]


def local(features, history, batch_clusters, pull_list, halo_ref, in_ref, tiles, w_in, w_layers):
    owner = halo_ref.reshape(count)
    slots = jnp.arange(devices, dtype=jnp.int32)
    spot = jnp.sum(
        jnp.where(owner[:, None] == slots[None, :], pull_list.reshape(1, devices), 0), axis=1
    )
    mine = jnp.pad(owner * count + spot, (0, lanes // 2 - count))
    mine = jnp.concatenate([mine, 4 * mine]).reshape(1, lanes)
    second, _, _, _, _, pushed = run_step(
        batch_clusters, 4 * invert(batch_clusters), in_ref, mine, features, history, tiles, w_in, w_layers
    )
    fresh, second_layer = place(pushed, second)
    return (second_layer, fresh)


def solution(mesh):
    placed = (
        P("dev", None),
        P("dev", None),
        P(),
        P("dev", None),
        P("dev", None),
        P("dev", None),
        P("dev", None, None, None),
        P(),
        P(),
    )
    return jax.shard_map(
        local,
        mesh=mesh,
        in_specs=placed,
        out_specs=(P("dev", None), P("dev", None)),
        check_vma=False,
    )
```

```python
import functools
import math

import jax
import jax.numpy as jnp
from jax import lax
from jax.experimental import pallas as pl
from jax.experimental.pallas import tpu as pltpu
from jax.sharding import PartitionSpec as P

restart = 0.1
strength = 0.5
lanes = 128
devices = 128
count = 48
rows = count * lanes
height = 4 * count
both = 2 * count
group = 4
span = group * lanes
piece = 64
pad = 8
vmem_bytes = 60 * 1024 * 1024
bf16 = jnp.bfloat16
f32 = jnp.float32
MESH = pl.DeviceIdType.MESH
IDS, FEAT_OUT, HIST_OUT, FEAT_IN, PUSH_OUT, HIST_IN, PUSH_IN = range(7)
WAYS = 7


def partner(me, k):
    z, x, y, core = me // 32, me // 8 % 4, me // 2 % 4, me % 2
    return (
        (z + k // 32) % 4 * 32 + (x + k // 8 % 4) % 4 * 8 + (y + k // 2 % 4) % 4 * 2 + (core + k % 2) % 2
    )


def order(me, i):
    return partner(me, i * (37 + 54 * (me % 2)) % devices)


def at(ref, slot, size):
    return ref.at[pl.ds(pl.multiple_of(slot * size, size), size)]


def wait_all(ref, size, sem):
    part = ref.at[pl.ds(0, size)]
    pltpu.make_async_copy(part, part, sem).wait()


def send(src, dst, sems, way, peer):
    pltpu.make_async_remote_copy(
        src_ref=src,
        dst_ref=dst,
        send_sem=sems.at[0, way],
        recv_sem=sems.at[1, way],
        device_id=(peer,),
        device_id_type=MESH,
    ).start()


def send_pieces(src_ref, src_slot, dst_ref, dst_slot, sems, way, peer):
    for part in range(height // piece):
        src = src_ref.at[pl.ds(pl.multiple_of(src_slot * height + part * piece, piece), piece)]
        dst = dst_ref.at[pl.ds(pl.multiple_of(dst_slot * height + part * piece, piece), piece)]
        send(src, dst, sems, way, peer)


def widen(src, dst, offset, size):
    chunk = 256

    def step(i, carry):
        here = pl.multiple_of(i * chunk, chunk)
        dst[pl.ds(offset + here, chunk), :] = src[pl.ds(here, chunk), :].astype(f32)
        return carry

    lax.fori_loop(0, size // chunk, step, 0)


def spread(src, dst, size, parts, offset=0):
    def step(i, carry):
        dst[pl.ds(pl.multiple_of((offset + i) * (size + pad), 8), size), :] = src[
            pl.ds(pl.multiple_of(i * size, size), size), :
        ].astype(f32)
        return carry

    lax.fori_loop(0, parts, step, 0, unroll=2)


def project(x, weight):
    return jnp.maximum(jnp.dot(x, weight, preferred_element_type=f32), 0.0).astype(bf16)


def mix(left, right, initial):
    aggregate = jnp.dot(left, right, preferred_element_type=f32)
    return (1.0 - restart) * aggregate + restart * initial.astype(f32)


def finish(support, weight, layer):
    mix_rate = math.log(strength / layer + 1.0)
    mixed = jnp.dot(support.astype(bf16), weight, preferred_element_type=f32)
    return jnp.maximum((1.0 - mix_rate) * support + mix_rate * mixed, 0.0).astype(bf16)


def step_body(
    batch_ref, own_ref, near, halo_ref, pull_ref, feat_ref, hist_ref, tile_ref, win_ref, w_ref,
    second, inputs, hist_mid, halo, push_mid, pushed,
    batch, mine_smem, mine, ids_mid, ids_smem, feat_wide, wide, stage, feat_send, feat_mid, inputs_send, given,
    wide_send, halo_send, state, support, tiles, ready, picked,
    sems, local_sem, stage_sem, tile_sem, out_sem,
):
    me = lax.axis_index("dev")

    def load_history(q):
        return pltpu.make_async_copy(
            hist_ref.at[:, pl.ds(q * lanes, lanes)], stage.at[q % 2], stage_sem.at[q % 2]
        )

    def load_part(src, q):
        return pltpu.make_async_copy(src.at[pl.ds(q * rows, rows)], stage.at[q % 2], stage_sem.at[q % 2])

    def load_wide(load, parts):
        for q in range(parts):
            load(q).wait()
            widen(stage.at[q % 2], wide, q * rows, rows)
            if q + 2 < parts:
                load(q + 2).start()

    def keep(src, src_slot, dst, dst_slot, size, way):
        return pltpu.make_async_copy(at(src, src_slot, size), at(dst, dst_slot, size), local_sem.at[way])

    def each(body, first, last):
        def step(i, carry):
            body(order(me, i))
            return carry

        lax.fori_loop(first, last, step, 0)

    load_tiles = pltpu.make_async_copy(tile_ref, tiles, tile_sem.at[0])
    load_batch = pltpu.make_async_copy(batch_ref, batch, tile_sem.at[1])
    barrier = pltpu.get_barrier_semaphore()

    def greet(i, carry):
        pl.semaphore_signal(barrier, inc=1, device_id=(partner(me, i),), device_id_type=MESH)
        return carry

    lax.fori_loop(1, devices, greet, 0)
    load_history(0).start()
    load_history(1).start()
    load_batch.start()
    spread(feat_ref, feat_wide, lanes, count)
    pl.semaphore_wait(barrier, devices - 1)

    def pack_feat(m):
        feat_send[pl.ds(pl.multiple_of(m * count, count), count), :] = feat_wide[
            pl.ds(m, count, stride=lanes + pad), :
        ].astype(bf16)

    def spread_feat(m):
        pack_feat(m)
        send(at(feat_send, m, count), at(feat_mid, me, count), sems, FEAT_OUT, m)

    each(spread_feat, 1, devices)
    pack_feat(me)
    keep_feat = keep(feat_send, me, feat_mid, me, count, FEAT_OUT)
    keep_feat.start()

    for b in range(count):
        slot = halo_ref[0, b]
        cluster = slot * count + pull_ref[0, slot]
        mine_smem[0, b] = cluster
        mine_smem[0, 64 + b] = 4 * cluster
        mine_smem[0, 128 + b] = 4 * own_ref[0, b]
    to_vmem = pltpu.make_async_copy(mine_smem, mine, local_sem.at[IDS])
    to_vmem.start()
    to_vmem.wait()
    each(lambda m: send(mine, ids_mid.at[me], sems, IDS, m), 1, devices)
    keep_ids = pltpu.make_async_copy(mine, ids_mid.at[me], local_sem.at[IDS])
    keep_ids.start()

    def pack_wide(m):
        wide_send[pl.ds(pl.multiple_of(m * height, height), height), :] = wide[
            pl.ds(m // 32 * rows + m % 32, height, stride=32), :
        ].astype(bf16)

    def spread_hist(m):
        pack_wide(m)
        send_pieces(wide_send, m, hist_mid, me, sems, HIST_OUT, m)

    load_wide(load_history, 4)
    load_tiles.start()
    pack_wide(me)
    keep_hist = keep(wide_send, me, hist_mid, me, height, HIST_OUT)
    keep_hist.start()
    each(spread_hist, 1, devices // 4)

    load_batch.wait()
    keep_ids.wait()
    wait_all(ids_mid, devices - 1, sems.at[1, IDS])
    to_smem = pltpu.make_async_copy(ids_mid, ids_smem, local_sem.at[IDS])
    to_smem.start()
    to_smem.wait()
    keep_feat.wait()
    wait_all(feat_mid, (devices - 1) * count, sems.at[1, FEAT_OUT])

    widen(feat_mid, feat_wide, 0, rows)

    def pick_feat(d):
        for b in range(count):
            picked[pl.ds(b, 1), :] = feat_wide[pl.ds(batch[b, d], 1), :]
        for b in range(count):
            picked[pl.ds(count + b, 1), :] = feat_wide[pl.ds(ids_smem[d, 0, b], 1), :]
        inputs_send[pl.ds(pl.multiple_of(d * both, both), both), :] = picked[pl.ds(0, both), :].astype(bf16)

    def serve_feat(d):
        pick_feat(d)
        send(at(inputs_send, d, both), at(inputs, me, both), sems, FEAT_IN, d)

    each(serve_feat, 1, devices)
    pick_feat(me)
    keep_inputs = keep(inputs_send, me, inputs, me, both, FEAT_IN)
    keep_inputs.start()
    each(spread_hist, devices // 4, devices)

    keep_inputs.wait()
    wait_all(inputs, (devices - 1) * both, sems.at[1, FEAT_IN])
    load_inputs = functools.partial(load_part, inputs)
    load_inputs(0).start()
    load_inputs(1).start()
    for q in range(2):
        load_inputs(q).wait()
        spread(stage.at[q], wide, both, devices // 2, q * (devices // 2))

    def order_inputs(b, carry):
        given[b] = wide[pl.ds(b, lanes, stride=both + pad), :].astype(bf16)
        return carry

    lax.fori_loop(0, both, order_inputs, 0, unroll=2)
    load_tiles.wait()

    def tile_row(b):
        return jnp.concatenate([tiles[b, 0], tiles[b, 1], tiles[b, 2]], axis=1)

    def first_group(g, carry):
        for k in range(group):
            b = g * group + k
            states = project(
                jnp.concatenate([given[b], given[near[0, b]], given[count + b]], axis=0),
                win_ref[...],
            )
            support[pl.ds(k * lanes, lanes), :] = mix(tile_row(b), states, states[:lanes])
        made = finish(support[...], w_ref[0], 1)
        for k in range(group):
            state[g * group + k] = made[k * lanes : (k + 1) * lanes]
        for q in range(4):
            wide[pl.ds(pl.multiple_of(q * rows + g * span, span), span), :] = made[
                :, q * lanes : (q + 1) * lanes
            ].astype(f32)
        return carry

    lax.fori_loop(0, count // group, first_group, 0)

    keep_hist.wait()
    wait_all(hist_mid, (devices - 1) * height, sems.at[0, HIST_OUT])

    def spread_push(m):
        pack_wide(m)
        send_pieces(wide_send, m, push_mid, me, sems, PUSH_OUT, m)

    each(spread_push, 1, devices)
    pack_wide(me)
    keep_push = keep(wide_send, me, push_mid, me, height, PUSH_OUT)
    keep_push.start()

    wait_all(hist_mid, (devices - 1) * height, sems.at[1, HIST_OUT])
    load_mid = functools.partial(load_part, hist_mid)
    load_mid(0).start()
    load_mid(1).start()
    load_wide(load_mid, 4)

    def pick_wide(dst, d, index):
        for b in range(count):
            picked[pl.ds(4 * b, 4), :] = wide[pl.ds(index(b), 4), :]
        dst[pl.ds(pl.multiple_of(d * height, height), height), :] = picked[...].astype(bf16)

    def pick_halo(d):
        pick_wide(halo_send, d, lambda b: ids_smem[d, 0, 64 + b])

    def serve_halo(d):
        pick_halo(d)
        send_pieces(halo_send, d, halo, me, sems, HIST_IN, d)

    each(serve_halo, 1, devices)
    pick_halo(me)
    keep_halo = keep(halo_send, me, halo, me, height, HIST_IN)
    keep_halo.start()

    keep_push.wait()
    wait_all(push_mid, (devices - 1) * height, sems.at[1, PUSH_OUT])
    load_push = functools.partial(load_part, push_mid)
    load_push(0).start()
    load_push(1).start()
    wait_all(push_mid, (devices - 1) * height, sems.at[0, PUSH_OUT])
    load_wide(load_push, 4)

    def pick_push(o):
        pick_wide(wide_send, o, lambda p: ids_smem[o, 0, 128 + p])

    def serve_push(o):
        pick_push(o)
        send_pieces(wide_send, o, pushed, me, sems, PUSH_IN, o)

    each(serve_push, 1, devices)
    pick_push(me)
    keep_pushed = keep(wide_send, me, pushed, me, height, PUSH_IN)
    keep_pushed.start()

    keep_halo.wait()
    wait_all(halo, (devices - 1) * height, sems.at[1, HIST_IN])
    load_halo = functools.partial(load_part, halo)
    load_halo(0).start()
    load_halo(1).start()
    load_wide(load_halo, 4)

    def halo_block(b):
        return jnp.concatenate(
            [
                jnp.concatenate(
                    [wide[pl.ds(q * rows + 4 * b + i, 32, stride=height), :] for i in range(4)], axis=0
                )
                for q in range(4)
            ],
            axis=1,
        ).astype(bf16)

    def write(g, slot):
        return pltpu.make_async_copy(
            ready.at[slot], second.at[pl.ds(pl.multiple_of(g * span, span), span)], out_sem.at[slot]
        )

    def second_pair(pair, carry):
        for slot in range(2):
            g = pair * 2 + slot
            for k in range(group):
                b = g * group + k
                initial = project(given[b], win_ref[...])
                states = jnp.concatenate([state[b], state[near[0, b]], halo_block(b)], axis=0)
                support[pl.ds(k * lanes, lanes), :] = mix(tile_row(b), states, initial)
            made = finish(support[...], w_ref[1], 2)

            @pl.when(pair > 0)
            def _():
                write(g - 2, slot).wait()

            ready[slot] = made
            write(g, slot).start()
        return carry

    lax.fori_loop(0, count // group // 2, second_pair, 0)
    for slot in range(2):
        write(count // group - 2 + slot, slot).wait()

    keep_pushed.wait()
    wait_all(pushed, (devices - 1) * height, sems.at[1, PUSH_IN])
    wait_all(ids_mid, devices - 1, sems.at[0, IDS])
    wait_all(feat_mid, (devices - 1) * count, sems.at[0, FEAT_OUT])
    wait_all(inputs, (devices - 1) * both, sems.at[0, FEAT_IN])
    wait_all(halo, (devices - 1) * height, sems.at[0, HIST_IN])
    wait_all(pushed, (devices - 1) * height, sems.at[0, PUSH_IN])


def run_step(batch, own, near, halo, pull, features, history, tiles, w_in, w_layers):
    anywhere = pl.BlockSpec(memory_space=pl.ANY)
    smem = pl.BlockSpec(memory_space=pltpu.SMEM)
    vmem = pl.BlockSpec(memory_space=pltpu.VMEM)
    shape = lambda *dims: jax.ShapeDtypeStruct(dims, bf16)
    sliced = shape(4 * rows, lanes)
    return pl.pallas_call(
        step_body,
        in_specs=[anywhere, smem, smem, smem, smem, vmem, anywhere, anywhere, vmem, vmem],
        out_specs=[anywhere] * 6,
        out_shape=[shape(rows, 4 * lanes), shape(2 * rows, lanes), sliced, sliced, sliced, sliced],
        scratch_shapes=[
            pltpu.SMEM((count, devices), jnp.int32),
            pltpu.SMEM((1, 2 * lanes), jnp.int32),
            pltpu.VMEM((1, 2 * lanes), jnp.int32),
            pltpu.VMEM((devices, 1, 2 * lanes), jnp.int32),
            pltpu.SMEM((devices, 1, 2 * lanes), jnp.int32),
            pltpu.VMEM((count * (lanes + pad), lanes), f32),
            pltpu.VMEM((4 * rows, lanes), f32),
            pltpu.VMEM((2, rows, lanes), bf16),
            pltpu.VMEM((rows, lanes), bf16),
            pltpu.VMEM((rows, lanes), bf16),
            pltpu.VMEM((2 * rows, lanes), bf16),
            pltpu.VMEM((both, lanes, lanes), bf16),
            pltpu.VMEM((4 * rows, lanes), bf16),
            pltpu.VMEM((4 * rows, lanes), bf16),
            pltpu.VMEM((count, lanes, 4 * lanes), bf16),
            pltpu.VMEM((span, 4 * lanes), f32),
            pltpu.VMEM((count, 3, lanes, lanes), bf16),
            pltpu.VMEM((2, span, 4 * lanes), bf16),
            pltpu.VMEM((height, lanes), f32),
            pltpu.SemaphoreType.DMA((2, WAYS)),
            pltpu.SemaphoreType.DMA((WAYS,)),
            pltpu.SemaphoreType.DMA((2,)),
            pltpu.SemaphoreType.DMA((2,)),
            pltpu.SemaphoreType.DMA((2,)),
        ],
        compiler_params=pltpu.CompilerParams(
            vmem_limit_bytes=vmem_bytes, collective_id=1, has_side_effects=True
        ),
        cost_estimate=pl.CostEstimate(flops=14_000_000_000, bytes_accessed=100_000_000, transcendentals=0),
    )(batch, own, near, halo, pull, features, history, tiles, w_in, w_layers)


def place_body(pushed, second, fresh, result, wide):
    result[...] = second[...]
    spread(pushed, wide, height, 32)

    def move(a, carry):
        fresh[pl.ds(pl.multiple_of(a * 32, 32), 32), :] = wide[
            pl.ds(a, 32, stride=height + pad), :
        ].astype(bf16)
        return carry

    lax.fori_loop(0, height, move, 0, unroll=8)


def place(pushed, second):
    full = jax.ShapeDtypeStruct((rows, 4 * lanes), bf16)
    quarter = pl.BlockSpec((rows // 4, 4 * lanes), lambda q: (q, 0))
    return pl.pallas_call(
        place_body,
        grid=(4,),
        in_specs=[pl.BlockSpec((rows, lanes), lambda q: (q, 0)), quarter],
        out_specs=[pl.BlockSpec((rows, lanes), lambda q: (0, q)), quarter],
        out_shape=[full, full],
        scratch_shapes=[pltpu.VMEM((32 * (height + pad), lanes), f32)],
        compiler_params=pltpu.CompilerParams(vmem_limit_bytes=vmem_bytes),
        cost_estimate=pl.CostEstimate(flops=0, bytes_accessed=40_000_000, transcendentals=0),
    )(pushed, second)


def own_places(batch):
    spot = jnp.arange(batch.size, dtype=jnp.int32).reshape(batch.shape)[:, :, None]
    cluster = lax.axis_index("dev") * count + jnp.arange(count, dtype=jnp.int32)
    return jnp.sum(jnp.where(batch[:, :, None] == cluster, spot, 0), axis=(0, 1)).reshape(1, count)


def local(features, history, batch_clusters, pull_list, halo_ref, in_ref, tiles, w_in, w_layers):
    second, _, _, _, _, pushed = run_step(
        batch_clusters.T, own_places(batch_clusters), in_ref, halo_ref, pull_list,
        features, history, tiles, w_in, w_layers,
    )
    fresh, second_layer = place(pushed, second)
    return (second_layer, fresh)


def solution(mesh):
    placed = (
        P("dev", None),
        P("dev", None),
        P(),
        P("dev", None),
        P("dev", None),
        P("dev", None),
        P("dev", None, None, None),
        P(),
        P(),
    )
    return jax.shard_map(
        local,
        mesh=mesh,
        in_specs=placed,
        out_specs=(P("dev", None), P("dev", None)),
        check_vma=False,
    )
```

```python
import functools
import math

import jax
import jax.numpy as jnp
from jax import lax
from jax.experimental import pallas as pl
from jax.experimental.pallas import tpu as pltpu
from jax.sharding import PartitionSpec as P

restart = 0.1
strength = 0.5
lanes = 128
devices = 128
count = 48
rows = count * lanes
height = 4 * count
both = 2 * count
group = 4
span = group * lanes
piece = 64
pad = 8
vmem_bytes = 60 * 1024 * 1024
bf16 = jnp.bfloat16
f32 = jnp.float32
MESH = pl.DeviceIdType.MESH
IDS, FEAT_OUT, HIST_OUT, FEAT_IN, PUSH_OUT, HIST_IN, PUSH_IN = range(7)
WAYS = 7

turns = ((37, 91), (37, 91), (91, 37), (45, 83), (83, 45), (53, 75), (75, 53))


def partner(me, k):
    z, x, y, core = me // 32, me // 8 % 4, me // 2 % 4, me % 2
    return (
        (z + k // 32) % 4 * 32 + (x + k // 8 % 4) % 4 * 8 + (y + k // 2 % 4) % 4 * 2 + (core + k % 2) % 2
    )


def order(me, i, way):
    first, second = turns[way]
    step = first + (second - first) * (me % 2)
    return partner(me, i * step % devices)


def at(ref, slot, size):
    return ref.at[pl.ds(pl.multiple_of(slot * size, size), size)]


def wait_all(ref, size, sem):
    part = ref.at[pl.ds(0, size)]
    pltpu.make_async_copy(part, part, sem).wait()


def send(src, dst, sems, way, peer):
    pltpu.make_async_remote_copy(
        src_ref=src,
        dst_ref=dst,
        send_sem=sems.at[0, way],
        recv_sem=sems.at[1, way],
        device_id=(peer,),
        device_id_type=MESH,
    ).start()


def send_pieces(src_ref, src_slot, dst_ref, dst_slot, sems, way, peer, parts=range(height // piece)):
    for part in parts:
        src = src_ref.at[pl.ds(pl.multiple_of(src_slot * height + part * piece, piece), piece)]
        dst = dst_ref.at[pl.ds(pl.multiple_of(dst_slot * height + part * piece, piece), piece)]
        send(src, dst, sems, way, peer)


def widen(src, dst, offset, size):
    chunk = 256

    def step(i, carry):
        here = pl.multiple_of(i * chunk, chunk)
        dst[pl.ds(offset + here, chunk), :] = src[pl.ds(here, chunk), :].astype(f32)
        return carry

    lax.fori_loop(0, size // chunk, step, 0)


def spread(src, dst, size, parts, offset=0):
    def step(i, carry):
        dst[pl.ds(pl.multiple_of((offset + i) * (size + pad), 8), size), :] = src[
            pl.ds(pl.multiple_of(i * size, size), size), :
        ].astype(f32)
        return carry

    lax.fori_loop(0, parts, step, 0, unroll=2)


def project(x, weight):
    return jnp.maximum(jnp.dot(x, weight, preferred_element_type=f32), 0.0).astype(bf16)


def mix(left, right, initial):
    aggregate = jnp.dot(left, right, preferred_element_type=f32)
    return (1.0 - restart) * aggregate + restart * initial.astype(f32)


def finish(support, weight, layer):
    mix_rate = math.log(strength / layer + 1.0)
    mixed = jnp.dot(support.astype(bf16), weight, preferred_element_type=f32)
    return jnp.maximum((1.0 - mix_rate) * support + mix_rate * mixed, 0.0).astype(bf16)


def step_body(
    batch_ref, own_ref, near, halo_ref, pull_ref, feat_ref, hist_ref, tile_ref, win_ref, w_ref,
    second, inputs, hist_mid, halo, push_mid, pushed,
    batch, mine_smem, mine, ids_mid, ids_smem, feat_wide, wide, stage, feat_send, feat_mid, inputs_send, given,
    wide_send, halo_send, state, support, tiles, ready, picked,
    sems, local_sem, stage_sem, tile_sem, out_sem,
):
    me = lax.axis_index("dev")

    def load_history(q):
        return pltpu.make_async_copy(
            hist_ref.at[:, pl.ds(q * lanes, lanes)], stage.at[q % 2], stage_sem.at[q % 2]
        )

    def load_part(src, q):
        return pltpu.make_async_copy(src.at[pl.ds(q * rows, rows)], stage.at[q % 2], stage_sem.at[q % 2])

    def load_wide(load, parts):
        for q in range(parts):
            load(q).wait()
            widen(stage.at[q % 2], wide, q * rows, rows)
            if q + 2 < parts:
                load(q + 2).start()

    def keep(src, src_slot, dst, dst_slot, size, way):
        return pltpu.make_async_copy(at(src, src_slot, size), at(dst, dst_slot, size), local_sem.at[way])

    def each(way, body, first, last):
        def step(i, carry):
            body(order(me, i, way))
            return carry

        lax.fori_loop(first, last, step, 0)

    load_tiles = pltpu.make_async_copy(tile_ref, tiles, tile_sem.at[0])
    load_batch = pltpu.make_async_copy(batch_ref, batch, tile_sem.at[1])
    barrier = pltpu.get_barrier_semaphore()

    def greet(i, carry):
        pl.semaphore_signal(barrier, inc=1, device_id=(partner(me, i),), device_id_type=MESH)
        return carry

    lax.fori_loop(1, devices, greet, 0)
    load_history(0).start()
    load_history(1).start()
    load_batch.start()
    spread(feat_ref, feat_wide, lanes, count)
    pl.semaphore_wait(barrier, devices - 1)

    def pack_feat(m):
        feat_send[pl.ds(pl.multiple_of(m * count, count), count), :] = feat_wide[
            pl.ds(m, count, stride=lanes + pad), :
        ].astype(bf16)

    def spread_feat(m):
        pack_feat(m)
        send(at(feat_send, m, count), at(feat_mid, me, count), sems, FEAT_OUT, m)

    each(FEAT_OUT, spread_feat, 1, devices)
    pack_feat(me)
    keep_feat = keep(feat_send, me, feat_mid, me, count, FEAT_OUT)
    keep_feat.start()

    for b in range(count):
        slot = halo_ref[0, b]
        cluster = slot * count + pull_ref[0, slot]
        mine_smem[0, b] = cluster
        mine_smem[0, 64 + b] = 4 * cluster
        mine_smem[0, 128 + b] = 4 * own_ref[0, b]
    to_vmem = pltpu.make_async_copy(mine_smem, mine, local_sem.at[IDS])
    to_vmem.start()
    to_vmem.wait()
    each(IDS, lambda m: send(mine, ids_mid.at[me], sems, IDS, m), 1, devices)
    keep_ids = pltpu.make_async_copy(mine, ids_mid.at[me], local_sem.at[IDS])
    keep_ids.start()

    def pack_wide(m):
        wide_send[pl.ds(pl.multiple_of(m * height, height), height), :] = wide[
            pl.ds(m // 32 * rows + m % 32, height, stride=32), :
        ].astype(bf16)

    def spread_hist(m):
        pack_wide(m)
        send_pieces(wide_send, m, hist_mid, me, sems, HIST_OUT, m)

    load_wide(load_history, 4)
    load_tiles.start()
    pack_wide(me)
    keep_hist = keep(wide_send, me, hist_mid, me, height, HIST_OUT)
    keep_hist.start()
    each(HIST_OUT, spread_hist, 1, devices // 4)

    load_batch.wait()
    keep_ids.wait()
    wait_all(ids_mid, devices - 1, sems.at[1, IDS])
    to_smem = pltpu.make_async_copy(ids_mid, ids_smem, local_sem.at[IDS])
    to_smem.start()
    to_smem.wait()
    keep_feat.wait()
    wait_all(feat_mid, (devices - 1) * count, sems.at[1, FEAT_OUT])

    widen(feat_mid, feat_wide, 0, rows)

    def pick_feat(d):
        for b in range(count):
            picked[pl.ds(b, 1), :] = feat_wide[pl.ds(batch[b, d], 1), :]
        for b in range(count):
            picked[pl.ds(count + b, 1), :] = feat_wide[pl.ds(ids_smem[d, 0, b], 1), :]
        inputs_send[pl.ds(pl.multiple_of(d * both, both), both), :] = picked[pl.ds(0, both), :].astype(bf16)

    def serve_feat(d):
        pick_feat(d)
        send(at(inputs_send, d, both), at(inputs, me, both), sems, FEAT_IN, d)

    each(FEAT_IN, serve_feat, 1, devices)
    pick_feat(me)
    keep_inputs = keep(inputs_send, me, inputs, me, both, FEAT_IN)
    keep_inputs.start()
    each(HIST_OUT, spread_hist, devices // 4, devices)

    keep_inputs.wait()
    wait_all(inputs, (devices - 1) * both, sems.at[1, FEAT_IN])
    load_inputs = functools.partial(load_part, inputs)
    load_inputs(0).start()
    load_inputs(1).start()
    for q in range(2):
        load_inputs(q).wait()
        spread(stage.at[q], wide, both, devices // 2, q * (devices // 2))

    def order_inputs(b, carry):
        given[b] = wide[pl.ds(b, lanes, stride=both + pad), :].astype(bf16)
        return carry

    lax.fori_loop(0, both, order_inputs, 0, unroll=2)
    load_tiles.wait()

    def tile_row(b):
        return jnp.concatenate([tiles[b, 0], tiles[b, 1], tiles[b, 2]], axis=1)

    def first_group(g, carry):
        for k in range(group):
            b = g * group + k
            states = project(
                jnp.concatenate([given[b], given[near[0, b]], given[count + b]], axis=0),
                win_ref[...],
            )
            support[pl.ds(k * lanes, lanes), :] = mix(tile_row(b), states, states[:lanes])
        made = finish(support[...], w_ref[0], 1)
        for k in range(group):
            state[g * group + k] = made[k * lanes : (k + 1) * lanes]
        for q in range(4):
            wide[pl.ds(pl.multiple_of(q * rows + g * span, span), span), :] = made[
                :, q * lanes : (q + 1) * lanes
            ].astype(f32)
        return carry

    lax.fori_loop(0, count // group, first_group, 0)

    keep_hist.wait()
    wait_all(hist_mid, (devices - 1) * height, sems.at[0, HIST_OUT])

    def spread_push(m):
        pack_wide(m)
        send_pieces(wide_send, m, push_mid, me, sems, PUSH_OUT, m, (0,))

    each(PUSH_OUT, spread_push, 1, devices)
    for part in range(1, height // piece):
        each(PUSH_OUT, lambda m: send_pieces(wide_send, m, push_mid, me, sems, PUSH_OUT, m, (part,)), 1, devices)
    pack_wide(me)
    keep_push = keep(wide_send, me, push_mid, me, height, PUSH_OUT)
    keep_push.start()

    wait_all(hist_mid, (devices - 1) * height, sems.at[1, HIST_OUT])
    load_mid = functools.partial(load_part, hist_mid)
    load_mid(0).start()
    load_mid(1).start()
    load_wide(load_mid, 4)

    def pick_wide(dst, d, index):
        for b in range(count):
            picked[pl.ds(4 * b, 4), :] = wide[pl.ds(index(b), 4), :]
        dst[pl.ds(pl.multiple_of(d * height, height), height), :] = picked[...].astype(bf16)

    def pick_halo(d):
        pick_wide(halo_send, d, lambda b: ids_smem[d, 0, 64 + b])

    def serve_halo(d):
        pick_halo(d)
        send_pieces(halo_send, d, halo, me, sems, HIST_IN, d, (0,))

    each(HIST_IN, serve_halo, 1, devices)
    for part in range(1, height // piece):
        each(HIST_IN, lambda d: send_pieces(halo_send, d, halo, me, sems, HIST_IN, d, (part,)), 1, devices)
    pick_halo(me)
    keep_halo = keep(halo_send, me, halo, me, height, HIST_IN)
    keep_halo.start()

    keep_push.wait()
    wait_all(push_mid, (devices - 1) * height, sems.at[1, PUSH_OUT])
    load_push = functools.partial(load_part, push_mid)
    load_push(0).start()
    load_push(1).start()
    wait_all(push_mid, (devices - 1) * height, sems.at[0, PUSH_OUT])
    load_wide(load_push, 4)

    def pick_push(o):
        pick_wide(wide_send, o, lambda p: ids_smem[o, 0, 128 + p])

    def serve_push(o):
        pick_push(o)
        send_pieces(wide_send, o, pushed, me, sems, PUSH_IN, o, (0,))

    each(PUSH_IN, serve_push, 1, devices)
    for part in range(1, height // piece):
        each(PUSH_IN, lambda o: send_pieces(wide_send, o, pushed, me, sems, PUSH_IN, o, (part,)), 1, devices)
    pick_push(me)
    keep_pushed = keep(wide_send, me, pushed, me, height, PUSH_IN)
    keep_pushed.start()

    keep_halo.wait()
    wait_all(halo, (devices - 1) * height, sems.at[1, HIST_IN])
    load_halo = functools.partial(load_part, halo)
    load_halo(0).start()
    load_halo(1).start()
    load_wide(load_halo, 4)

    def halo_block(b):
        return jnp.concatenate(
            [
                jnp.concatenate(
                    [wide[pl.ds(q * rows + 4 * b + i, 32, stride=height), :] for i in range(4)], axis=0
                )
                for q in range(4)
            ],
            axis=1,
        ).astype(bf16)

    def write(g, slot):
        return pltpu.make_async_copy(
            ready.at[slot], second.at[pl.ds(pl.multiple_of(g * span, span), span)], out_sem.at[slot]
        )

    def second_pair(pair, carry):
        for slot in range(2):
            g = pair * 2 + slot
            for k in range(group):
                b = g * group + k
                initial = project(given[b], win_ref[...])
                states = jnp.concatenate([state[b], state[near[0, b]], halo_block(b)], axis=0)
                support[pl.ds(k * lanes, lanes), :] = mix(tile_row(b), states, initial)
            made = finish(support[...], w_ref[1], 2)

            @pl.when(pair > 0)
            def _():
                write(g - 2, slot).wait()

            ready[slot] = made
            write(g, slot).start()
        return carry

    lax.fori_loop(0, count // group // 2, second_pair, 0)
    for slot in range(2):
        write(count // group - 2 + slot, slot).wait()

    keep_pushed.wait()
    wait_all(pushed, (devices - 1) * height, sems.at[1, PUSH_IN])
    wait_all(ids_mid, devices - 1, sems.at[0, IDS])
    wait_all(feat_mid, (devices - 1) * count, sems.at[0, FEAT_OUT])
    wait_all(inputs, (devices - 1) * both, sems.at[0, FEAT_IN])
    wait_all(halo, (devices - 1) * height, sems.at[0, HIST_IN])
    wait_all(pushed, (devices - 1) * height, sems.at[0, PUSH_IN])


def run_step(batch, own, near, halo, pull, features, history, tiles, w_in, w_layers):
    anywhere = pl.BlockSpec(memory_space=pl.ANY)
    smem = pl.BlockSpec(memory_space=pltpu.SMEM)
    vmem = pl.BlockSpec(memory_space=pltpu.VMEM)
    shape = lambda *dims: jax.ShapeDtypeStruct(dims, bf16)
    sliced = shape(4 * rows, lanes)
    return pl.pallas_call(
        step_body,
        in_specs=[anywhere, smem, smem, smem, smem, vmem, anywhere, anywhere, vmem, vmem],
        out_specs=[anywhere] * 6,
        out_shape=[shape(rows, 4 * lanes), shape(2 * rows, lanes), sliced, sliced, sliced, sliced],
        scratch_shapes=[
            pltpu.SMEM((count, devices), jnp.int32),
            pltpu.SMEM((1, 2 * lanes), jnp.int32),
            pltpu.VMEM((1, 2 * lanes), jnp.int32),
            pltpu.VMEM((devices, 1, 2 * lanes), jnp.int32),
            pltpu.SMEM((devices, 1, 2 * lanes), jnp.int32),
            pltpu.VMEM((count * (lanes + pad), lanes), f32),
            pltpu.VMEM((4 * rows, lanes), f32),
            pltpu.VMEM((2, rows, lanes), bf16),
            pltpu.VMEM((rows, lanes), bf16),
            pltpu.VMEM((rows, lanes), bf16),
            pltpu.VMEM((2 * rows, lanes), bf16),
            pltpu.VMEM((both, lanes, lanes), bf16),
            pltpu.VMEM((4 * rows, lanes), bf16),
            pltpu.VMEM((4 * rows, lanes), bf16),
            pltpu.VMEM((count, lanes, 4 * lanes), bf16),
            pltpu.VMEM((span, 4 * lanes), f32),
            pltpu.VMEM((count, 3, lanes, lanes), bf16),
            pltpu.VMEM((2, span, 4 * lanes), bf16),
            pltpu.VMEM((height, lanes), f32),
            pltpu.SemaphoreType.DMA((2, WAYS)),
            pltpu.SemaphoreType.DMA((WAYS,)),
            pltpu.SemaphoreType.DMA((2,)),
            pltpu.SemaphoreType.DMA((2,)),
            pltpu.SemaphoreType.DMA((2,)),
        ],
        compiler_params=pltpu.CompilerParams(
            vmem_limit_bytes=vmem_bytes, collective_id=1, has_side_effects=True
        ),
        cost_estimate=pl.CostEstimate(flops=14_000_000_000, bytes_accessed=100_000_000, transcendentals=0),
    )(batch, own, near, halo, pull, features, history, tiles, w_in, w_layers)


def place_body(pushed, second, fresh, result, wide):
    result[...] = second[...]
    spread(pushed, wide, height, 32)

    def move(a, carry):
        fresh[pl.ds(pl.multiple_of(a * 32, 32), 32), :] = wide[
            pl.ds(a, 32, stride=height + pad), :
        ].astype(bf16)
        return carry

    lax.fori_loop(0, height, move, 0, unroll=8)


def place(pushed, second):
    full = jax.ShapeDtypeStruct((rows, 4 * lanes), bf16)
    quarter = pl.BlockSpec((rows // 4, 4 * lanes), lambda q: (q, 0))
    return pl.pallas_call(
        place_body,
        grid=(4,),
        in_specs=[pl.BlockSpec((rows, lanes), lambda q: (q, 0)), quarter],
        out_specs=[pl.BlockSpec((rows, lanes), lambda q: (0, q)), quarter],
        out_shape=[full, full],
        scratch_shapes=[pltpu.VMEM((32 * (height + pad), lanes), f32)],
        compiler_params=pltpu.CompilerParams(vmem_limit_bytes=vmem_bytes),
        cost_estimate=pl.CostEstimate(flops=0, bytes_accessed=40_000_000, transcendentals=0),
    )(pushed, second)


def own_places(batch):
    spot = jnp.arange(batch.size, dtype=jnp.int32).reshape(batch.shape)[:, :, None]
    cluster = lax.axis_index("dev") * count + jnp.arange(count, dtype=jnp.int32)
    return jnp.sum(jnp.where(batch[:, :, None] == cluster, spot, 0), axis=(0, 1)).reshape(1, count)


def local(features, history, batch_clusters, pull_list, halo_ref, in_ref, tiles, w_in, w_layers):
    second, _, _, _, _, pushed = run_step(
        batch_clusters.T, own_places(batch_clusters), in_ref, halo_ref, pull_list,
        features, history, tiles, w_in, w_layers,
    )
    fresh, second_layer = place(pushed, second)
    return (second_layer, fresh)


def solution(mesh):
    placed = (
        P("dev", None),
        P("dev", None),
        P(),
        P("dev", None),
        P("dev", None),
        P("dev", None),
        P("dev", None, None, None),
        P(),
        P(),
    )
    return jax.shard_map(
        local,
        mesh=mesh,
        in_specs=placed,
        out_specs=(P("dev", None), P("dev", None)),
        check_vma=False,
    )
```

```python
import functools
import math

import jax
import jax.numpy as jnp
from jax import lax
from jax.experimental import pallas as pl
from jax.experimental.pallas import tpu as pltpu
from jax.sharding import PartitionSpec as P

restart = 0.1
strength = 0.5
lanes = 128
devices = 128
count = 48
rows = count * lanes
height = 4 * count
both = 2 * count
group = 4
span = group * lanes
piece = 64
pad = 8
vmem_bytes = 60 * 1024 * 1024
bf16 = jnp.bfloat16
f32 = jnp.float32
MESH = pl.DeviceIdType.MESH
IDS, FEAT_OUT, HIST_OUT, FEAT_IN, PUSH_OUT, HIST_IN, PUSH_IN = range(7)
WAYS = 7

turns = ((37, 91), (37, 91), (91, 37), (45, 83), (83, 45), (53, 75), (75, 53))


def partner(me, k):
    z, x, y, core = me // 32, me // 8 % 4, me // 2 % 4, me % 2
    return (
        (z + k // 32) % 4 * 32 + (x + k // 8 % 4) % 4 * 8 + (y + k // 2 % 4) % 4 * 2 + (core + k % 2) % 2
    )


def order(me, i, way):
    first, second = turns[way]
    step = first + (second - first) * (me % 2)
    return partner(me, i * step % devices)


def at(ref, slot, size):
    return ref.at[pl.ds(pl.multiple_of(slot * size, size), size)]


def wait_all(ref, size, sem):
    part = ref.at[pl.ds(0, size)]
    pltpu.make_async_copy(part, part, sem).wait()


def send(src, dst, sems, way, peer):
    pltpu.make_async_remote_copy(
        src_ref=src,
        dst_ref=dst,
        send_sem=sems.at[0, way],
        recv_sem=sems.at[1, way],
        device_id=(peer,),
        device_id_type=MESH,
    ).start()


def send_pieces(src_ref, src_slot, dst_ref, dst_slot, sems, way, peer, parts=range(height // piece)):
    for part in parts:
        src = src_ref.at[pl.ds(pl.multiple_of(src_slot * height + part * piece, piece), piece)]
        dst = dst_ref.at[pl.ds(pl.multiple_of(dst_slot * height + part * piece, piece), piece)]
        send(src, dst, sems, way, peer)


def widen(src, dst, offset, size):
    chunk = 256

    def step(i, carry):
        here = pl.multiple_of(i * chunk, chunk)
        dst[pl.ds(offset + here, chunk), :] = src[pl.ds(here, chunk), :].astype(f32)
        return carry

    lax.fori_loop(0, size // chunk, step, 0)


def spread(src, dst, size, parts, offset=0):
    def step(i, carry):
        dst[pl.ds(pl.multiple_of((offset + i) * (size + pad), 8), size), :] = src[
            pl.ds(pl.multiple_of(i * size, size), size), :
        ].astype(f32)
        return carry

    lax.fori_loop(0, parts, step, 0, unroll=2)


def project(x, weight):
    return jnp.maximum(jnp.dot(x, weight, preferred_element_type=f32), 0.0).astype(bf16)


def mix(left, right, initial):
    aggregate = jnp.dot(left, right, preferred_element_type=f32)
    return (1.0 - restart) * aggregate + restart * initial.astype(f32)


def finish(support, weight, layer):
    mix_rate = math.log(strength / layer + 1.0)
    mixed = jnp.dot(support.astype(bf16), weight, preferred_element_type=f32)
    return jnp.maximum((1.0 - mix_rate) * support + mix_rate * mixed, 0.0).astype(bf16)


def step_body(
    batch_ref, own_ref, near, halo_ref, pull_ref, feat_ref, hist_ref, tile_ref, win_ref, w_ref,
    second, inputs, hist_mid, halo, push_mid, pushed,
    batch, mine_smem, mine, ids_mid, ids_smem, feat_wide, wide, stage, feat_send, feat_mid, inputs_send, given,
    wide_send, halo_send, state, support, tiles, ready, picked,
    sems, local_sem, stage_sem, tile_sem, out_sem,
):
    me = lax.axis_index("dev")

    def load_history(q):
        return pltpu.make_async_copy(
            hist_ref.at[:, pl.ds(q * lanes, lanes)], stage.at[q % 2], stage_sem.at[q % 2]
        )

    def load_part(src, q):
        return pltpu.make_async_copy(src.at[pl.ds(q * rows, rows)], stage.at[q % 2], stage_sem.at[q % 2])

    def load_wide(load, parts):
        for q in range(parts):
            load(q).wait()
            widen(stage.at[q % 2], wide, q * rows, rows)
            if q + 2 < parts:
                load(q + 2).start()

    def keep(src, src_slot, dst, dst_slot, size, way):
        return pltpu.make_async_copy(at(src, src_slot, size), at(dst, dst_slot, size), local_sem.at[way])

    def each(way, body, first, last):
        def step(i, carry):
            body(order(me, i, way))
            return carry

        lax.fori_loop(first, last, step, 0)

    load_tiles = pltpu.make_async_copy(tile_ref, tiles, tile_sem.at[0])
    load_batch = pltpu.make_async_copy(batch_ref, batch, tile_sem.at[1])
    barrier = pltpu.get_barrier_semaphore()

    def greet(i, carry):
        pl.semaphore_signal(barrier, inc=1, device_id=(partner(me, i),), device_id_type=MESH)
        return carry

    lax.fori_loop(1, devices, greet, 0)
    load_history(0).start()
    load_history(1).start()
    load_batch.start()
    for b in range(count):
        slot = halo_ref[0, b]
        cluster = slot * count + pull_ref[0, slot]
        mine_smem[0, b] = cluster
        mine_smem[0, 64 + b] = 4 * cluster
        mine_smem[0, 128 + b] = 4 * own_ref[0, b]
    to_vmem = pltpu.make_async_copy(mine_smem, mine, local_sem.at[IDS])
    to_vmem.start()
    spread(feat_ref, feat_wide, lanes, count)
    pl.semaphore_wait(barrier, devices - 1)

    def pack_feat(m):
        feat_send[pl.ds(pl.multiple_of(m * count, count), count), :] = feat_wide[
            pl.ds(m, count, stride=lanes + pad), :
        ].astype(bf16)

    def spread_feat(m):
        pack_feat(m)
        send(at(feat_send, m, count), at(feat_mid, me, count), sems, FEAT_OUT, m)

    each(FEAT_OUT, spread_feat, 1, devices)
    pack_feat(me)
    keep_feat = keep(feat_send, me, feat_mid, me, count, FEAT_OUT)
    keep_feat.start()

    def pack_wide(m):
        wide_send[pl.ds(pl.multiple_of(m * height, height), height), :] = wide[
            pl.ds(m // 32 * rows + m % 32, height, stride=32), :
        ].astype(bf16)

    def spread_hist(m):
        pack_wide(m)
        send_pieces(wide_send, m, hist_mid, me, sems, HIST_OUT, m, (0,))

    def spread_rest(first, last):
        for part in range(1, height // piece):
            each(HIST_OUT, lambda m: send_pieces(wide_send, m, hist_mid, me, sems, HIST_OUT, m, (part,)), first, last)

    load_wide(load_history, 4)
    load_tiles.start()
    pack_wide(me)
    keep_hist = keep(wide_send, me, hist_mid, me, height, HIST_OUT)
    keep_hist.start()
    each(HIST_OUT, spread_hist, 1, 8)
    to_vmem.wait()
    each(IDS, lambda m: send(mine, ids_mid.at[me], sems, IDS, m), 1, devices)
    keep_ids = pltpu.make_async_copy(mine, ids_mid.at[me], local_sem.at[IDS])
    keep_ids.start()
    each(HIST_OUT, spread_hist, 8, devices // 4)
    spread_rest(1, devices // 4)

    load_batch.wait()
    keep_ids.wait()
    wait_all(ids_mid, devices - 1, sems.at[1, IDS])
    to_smem = pltpu.make_async_copy(ids_mid, ids_smem, local_sem.at[IDS])
    to_smem.start()
    to_smem.wait()
    keep_feat.wait()
    wait_all(feat_mid, (devices - 1) * count, sems.at[1, FEAT_OUT])

    widen(feat_mid, feat_wide, 0, rows)

    def pick_feat(d):
        for b in range(count):
            picked[pl.ds(b, 1), :] = feat_wide[pl.ds(batch[b, d], 1), :]
        for b in range(count):
            picked[pl.ds(count + b, 1), :] = feat_wide[pl.ds(ids_smem[d, 0, b], 1), :]
        inputs_send[pl.ds(pl.multiple_of(d * both, both), both), :] = picked[pl.ds(0, both), :].astype(bf16)

    def serve_feat(d):
        pick_feat(d)
        send(at(inputs_send, d, both), at(inputs, me, both), sems, FEAT_IN, d)

    each(FEAT_IN, serve_feat, 1, devices)
    pick_feat(me)
    keep_inputs = keep(inputs_send, me, inputs, me, both, FEAT_IN)
    keep_inputs.start()
    each(HIST_OUT, spread_hist, devices // 4, devices)
    spread_rest(devices // 4, devices)

    keep_inputs.wait()
    wait_all(inputs, (devices - 1) * both, sems.at[1, FEAT_IN])
    load_inputs = functools.partial(load_part, inputs)
    load_inputs(0).start()
    load_inputs(1).start()
    for q in range(2):
        load_inputs(q).wait()
        spread(stage.at[q], wide, both, devices // 2, q * (devices // 2))

    def order_inputs(b, carry):
        given[b] = wide[pl.ds(b, lanes, stride=both + pad), :].astype(bf16)
        return carry

    lax.fori_loop(0, both, order_inputs, 0, unroll=2)
    load_tiles.wait()

    def tile_row(b):
        return jnp.concatenate([tiles[b, 0], tiles[b, 1], tiles[b, 2]], axis=1)

    def first_group(g, carry):
        for k in range(group):
            b = g * group + k
            states = project(
                jnp.concatenate([given[b], given[near[0, b]], given[count + b]], axis=0),
                win_ref[...],
            )
            support[pl.ds(k * lanes, lanes), :] = mix(tile_row(b), states, states[:lanes])
        made = finish(support[...], w_ref[0], 1)
        for k in range(group):
            state[g * group + k] = made[k * lanes : (k + 1) * lanes]
        for q in range(4):
            wide[pl.ds(pl.multiple_of(q * rows + g * span, span), span), :] = made[
                :, q * lanes : (q + 1) * lanes
            ].astype(f32)
        return carry

    lax.fori_loop(0, count // group, first_group, 0)

    keep_hist.wait()
    wait_all(hist_mid, (devices - 1) * height, sems.at[0, HIST_OUT])

    def spread_push(m):
        pack_wide(m)
        send_pieces(wide_send, m, push_mid, me, sems, PUSH_OUT, m, (0,))

    each(PUSH_OUT, spread_push, 1, devices)
    for part in range(1, height // piece):
        each(PUSH_OUT, lambda m: send_pieces(wide_send, m, push_mid, me, sems, PUSH_OUT, m, (part,)), 1, devices)
    pack_wide(me)
    keep_push = keep(wide_send, me, push_mid, me, height, PUSH_OUT)
    keep_push.start()

    wait_all(hist_mid, (devices - 1) * height, sems.at[1, HIST_OUT])
    load_mid = functools.partial(load_part, hist_mid)
    load_mid(0).start()
    load_mid(1).start()
    load_wide(load_mid, 4)

    def pick_wide(dst, d, index):
        for b in range(count):
            picked[pl.ds(4 * b, 4), :] = wide[pl.ds(index(b), 4), :]
        dst[pl.ds(pl.multiple_of(d * height, height), height), :] = picked[...].astype(bf16)

    def pick_halo(d):
        pick_wide(halo_send, d, lambda b: ids_smem[d, 0, 64 + b])

    def serve_halo(d):
        pick_halo(d)
        send_pieces(halo_send, d, halo, me, sems, HIST_IN, d, (0,))

    each(HIST_IN, serve_halo, 1, devices)
    for part in range(1, height // piece):
        each(HIST_IN, lambda d: send_pieces(halo_send, d, halo, me, sems, HIST_IN, d, (part,)), 1, devices)
    pick_halo(me)
    keep_halo = keep(halo_send, me, halo, me, height, HIST_IN)
    keep_halo.start()

    keep_push.wait()
    wait_all(push_mid, (devices - 1) * height, sems.at[1, PUSH_OUT])
    load_push = functools.partial(load_part, push_mid)
    load_push(0).start()
    load_push(1).start()
    wait_all(push_mid, (devices - 1) * height, sems.at[0, PUSH_OUT])
    load_wide(load_push, 4)

    def pick_push(o):
        pick_wide(wide_send, o, lambda p: ids_smem[o, 0, 128 + p])

    def serve_push(o):
        pick_push(o)
        send_pieces(wide_send, o, pushed, me, sems, PUSH_IN, o, (0,))

    each(PUSH_IN, serve_push, 1, devices)
    for part in range(1, height // piece):
        each(PUSH_IN, lambda o: send_pieces(wide_send, o, pushed, me, sems, PUSH_IN, o, (part,)), 1, devices)
    pick_push(me)
    keep_pushed = keep(wide_send, me, pushed, me, height, PUSH_IN)
    keep_pushed.start()

    keep_halo.wait()
    wait_all(halo, (devices - 1) * height, sems.at[1, HIST_IN])
    load_halo = functools.partial(load_part, halo)
    load_halo(0).start()
    load_halo(1).start()
    load_wide(load_halo, 4)

    def halo_block(b):
        return jnp.concatenate(
            [
                jnp.concatenate(
                    [wide[pl.ds(q * rows + 4 * b + i, 32, stride=height), :] for i in range(4)], axis=0
                )
                for q in range(4)
            ],
            axis=1,
        ).astype(bf16)

    def write(g, slot):
        return pltpu.make_async_copy(
            ready.at[slot], second.at[pl.ds(pl.multiple_of(g * span, span), span)], out_sem.at[slot]
        )

    def second_pair(pair, carry):
        for slot in range(2):
            g = pair * 2 + slot
            for k in range(group):
                b = g * group + k
                initial = project(given[b], win_ref[...])
                states = jnp.concatenate([state[b], state[near[0, b]], halo_block(b)], axis=0)
                support[pl.ds(k * lanes, lanes), :] = mix(tile_row(b), states, initial)
            made = finish(support[...], w_ref[1], 2)

            @pl.when(pair > 0)
            def _():
                write(g - 2, slot).wait()

            ready[slot] = made
            write(g, slot).start()
        return carry

    lax.fori_loop(0, count // group // 2, second_pair, 0)
    for slot in range(2):
        write(count // group - 2 + slot, slot).wait()

    keep_pushed.wait()
    wait_all(pushed, (devices - 1) * height, sems.at[1, PUSH_IN])
    wait_all(ids_mid, devices - 1, sems.at[0, IDS])
    wait_all(feat_mid, (devices - 1) * count, sems.at[0, FEAT_OUT])
    wait_all(inputs, (devices - 1) * both, sems.at[0, FEAT_IN])
    wait_all(halo, (devices - 1) * height, sems.at[0, HIST_IN])
    wait_all(pushed, (devices - 1) * height, sems.at[0, PUSH_IN])


def run_step(batch, own, near, halo, pull, features, history, tiles, w_in, w_layers):
    anywhere = pl.BlockSpec(memory_space=pl.ANY)
    smem = pl.BlockSpec(memory_space=pltpu.SMEM)
    vmem = pl.BlockSpec(memory_space=pltpu.VMEM)
    shape = lambda *dims: jax.ShapeDtypeStruct(dims, bf16)
    sliced = shape(4 * rows, lanes)
    return pl.pallas_call(
        step_body,
        in_specs=[anywhere, smem, smem, smem, smem, vmem, anywhere, anywhere, vmem, vmem],
        out_specs=[anywhere] * 6,
        out_shape=[shape(rows, 4 * lanes), shape(2 * rows, lanes), sliced, sliced, sliced, sliced],
        scratch_shapes=[
            pltpu.SMEM((count, devices), jnp.int32),
            pltpu.SMEM((1, 2 * lanes), jnp.int32),
            pltpu.VMEM((1, 2 * lanes), jnp.int32),
            pltpu.VMEM((devices, 1, 2 * lanes), jnp.int32),
            pltpu.SMEM((devices, 1, 2 * lanes), jnp.int32),
            pltpu.VMEM((count * (lanes + pad), lanes), f32),
            pltpu.VMEM((4 * rows, lanes), f32),
            pltpu.VMEM((2, rows, lanes), bf16),
            pltpu.VMEM((rows, lanes), bf16),
            pltpu.VMEM((rows, lanes), bf16),
            pltpu.VMEM((2 * rows, lanes), bf16),
            pltpu.VMEM((both, lanes, lanes), bf16),
            pltpu.VMEM((4 * rows, lanes), bf16),
            pltpu.VMEM((4 * rows, lanes), bf16),
            pltpu.VMEM((count, lanes, 4 * lanes), bf16),
            pltpu.VMEM((span, 4 * lanes), f32),
            pltpu.VMEM((count, 3, lanes, lanes), bf16),
            pltpu.VMEM((2, span, 4 * lanes), bf16),
            pltpu.VMEM((height, lanes), f32),
            pltpu.SemaphoreType.DMA((2, WAYS)),
            pltpu.SemaphoreType.DMA((WAYS,)),
            pltpu.SemaphoreType.DMA((2,)),
            pltpu.SemaphoreType.DMA((2,)),
            pltpu.SemaphoreType.DMA((2,)),
        ],
        compiler_params=pltpu.CompilerParams(
            vmem_limit_bytes=vmem_bytes, collective_id=1, has_side_effects=True
        ),
        cost_estimate=pl.CostEstimate(flops=14_000_000_000, bytes_accessed=100_000_000, transcendentals=0),
    )(batch, own, near, halo, pull, features, history, tiles, w_in, w_layers)


def place_body(pushed, second, fresh, result, wide):
    result[...] = second[...]
    spread(pushed, wide, height, 32)

    def move(a, carry):
        fresh[pl.ds(pl.multiple_of(a * 32, 32), 32), :] = wide[
            pl.ds(a, 32, stride=height + pad), :
        ].astype(bf16)
        return carry

    lax.fori_loop(0, height, move, 0, unroll=8)


def place(pushed, second):
    full = jax.ShapeDtypeStruct((rows, 4 * lanes), bf16)
    quarter = pl.BlockSpec((rows // 4, 4 * lanes), lambda q: (q, 0))
    return pl.pallas_call(
        place_body,
        grid=(4,),
        in_specs=[pl.BlockSpec((rows, lanes), lambda q: (q, 0)), quarter],
        out_specs=[pl.BlockSpec((rows, lanes), lambda q: (0, q)), quarter],
        out_shape=[full, full],
        scratch_shapes=[pltpu.VMEM((32 * (height + pad), lanes), f32)],
        compiler_params=pltpu.CompilerParams(vmem_limit_bytes=vmem_bytes),
        cost_estimate=pl.CostEstimate(flops=0, bytes_accessed=40_000_000, transcendentals=0),
    )(pushed, second)


def own_places(batch):
    spot = jnp.arange(batch.size, dtype=jnp.int32).reshape(batch.shape)[:, :, None]
    cluster = lax.axis_index("dev") * count + jnp.arange(count, dtype=jnp.int32)
    return jnp.sum(jnp.where(batch[:, :, None] == cluster, spot, 0), axis=(0, 1)).reshape(1, count)


def local(features, history, batch_clusters, pull_list, halo_ref, in_ref, tiles, w_in, w_layers):
    second, _, _, _, _, pushed = run_step(
        batch_clusters.T, own_places(batch_clusters), in_ref, halo_ref, pull_list,
        features, history, tiles, w_in, w_layers,
    )
    fresh, second_layer = place(pushed, second)
    return (second_layer, fresh)


def solution(mesh):
    placed = (
        P("dev", None),
        P("dev", None),
        P(),
        P("dev", None),
        P("dev", None),
        P("dev", None),
        P("dev", None, None, None),
        P(),
        P(),
    )
    return jax.shard_map(
        local,
        mesh=mesh,
        in_specs=placed,
        out_specs=(P("dev", None), P("dev", None)),
        check_vma=False,
    )
```

```python
import functools
import math

import jax
import jax.numpy as jnp
from jax import lax
from jax.experimental import pallas as pl
from jax.experimental.pallas import tpu as pltpu
from jax.sharding import PartitionSpec as P

restart = 0.1
strength = 0.5
lanes = 128
devices = 128
count = 48
rows = count * lanes
height = 4 * count
both = 2 * count
group = 4
span = group * lanes
piece = 64
pad = 8
vmem_bytes = 60 * 1024 * 1024
bf16 = jnp.bfloat16
f32 = jnp.float32
MESH = pl.DeviceIdType.MESH
IDS, FEAT_OUT, HIST_OUT, FEAT_IN, PUSH_OUT, HIST_IN, PUSH_IN = range(7)
WAYS = 7

turns = ((37, 91), (37, 91), (91, 37), (45, 83), (83, 45), (53, 75), (75, 53))


def partner(me, k):
    z, x, y, core = me // 32, me // 8 % 4, me // 2 % 4, me % 2
    return (
        (z + k // 32) % 4 * 32 + (x + k // 8 % 4) % 4 * 8 + (y + k // 2 % 4) % 4 * 2 + (core + k % 2) % 2
    )


def order(me, i, way):
    first, second = turns[way]
    step = first + (second - first) * (me % 2)
    return partner(me, i * step % devices)


def at(ref, slot, size):
    return ref.at[pl.ds(pl.multiple_of(slot * size, size), size)]


def wait_all(ref, size, sem):
    part = ref.at[pl.ds(0, size)]
    pltpu.make_async_copy(part, part, sem).wait()


def send(src, dst, sems, way, peer):
    pltpu.make_async_remote_copy(
        src_ref=src,
        dst_ref=dst,
        send_sem=sems.at[0, way],
        recv_sem=sems.at[1, way],
        device_id=(peer,),
        device_id_type=MESH,
    ).start()


def send_pieces(src_ref, src_slot, dst_ref, dst_slot, sems, way, peer, parts=range(height // piece)):
    for part in parts:
        src = src_ref.at[pl.ds(pl.multiple_of(src_slot * height + part * piece, piece), piece)]
        dst = dst_ref.at[pl.ds(pl.multiple_of(dst_slot * height + part * piece, piece), piece)]
        send(src, dst, sems, way, peer)


def widen(src, dst, offset, size):
    chunk = 256

    def step(i, carry):
        here = pl.multiple_of(i * chunk, chunk)
        dst[pl.ds(offset + here, chunk), :] = src[pl.ds(here, chunk), :].astype(f32)
        return carry

    lax.fori_loop(0, size // chunk, step, 0)


def spread(src, dst, size, parts, offset=0):
    def step(i, carry):
        dst[pl.ds(pl.multiple_of((offset + i) * (size + pad), 8), size), :] = src[
            pl.ds(pl.multiple_of(i * size, size), size), :
        ].astype(f32)
        return carry

    lax.fori_loop(0, parts, step, 0, unroll=2)


def project(x, weight):
    return jnp.maximum(jnp.dot(x, weight, preferred_element_type=f32), 0.0).astype(bf16)


def mix(left, right, initial):
    aggregate = jnp.dot(left, right, preferred_element_type=f32)
    return (1.0 - restart) * aggregate + restart * initial.astype(f32)


def finish(support, weight, layer):
    mix_rate = math.log(strength / layer + 1.0)
    mixed = jnp.dot(support.astype(bf16), weight, preferred_element_type=f32)
    return jnp.maximum((1.0 - mix_rate) * support + mix_rate * mixed, 0.0).astype(bf16)


def step_body(
    batch_ref, own_ref, near, halo_ref, pull_ref, feat_ref, hist_ref, tile_ref, win_ref, w_ref,
    second, inputs, hist_mid, halo, push_mid, pushed,
    batch, mine_smem, mine, ids_mid, ids_smem, feat_wide, wide, stage, feat_send, feat_mid, inputs_send, given,
    wide_send, halo_send, state, support, tiles, ready, picked,
    sems, local_sem, stage_sem, tile_sem, out_sem,
):
    me = lax.axis_index("dev")

    def load_history(q):
        return pltpu.make_async_copy(
            hist_ref.at[:, pl.ds(q * lanes, lanes)], stage.at[q % 2], stage_sem.at[q % 2]
        )

    def load_part(src, q):
        return pltpu.make_async_copy(src.at[pl.ds(q * rows, rows)], stage.at[q % 2], stage_sem.at[q % 2])

    def load_wide(load, parts):
        for q in range(parts):
            load(q).wait()
            widen(stage.at[q % 2], wide, q * rows, rows)
            if q + 2 < parts:
                load(q + 2).start()

    def keep(src, src_slot, dst, dst_slot, size, way):
        return pltpu.make_async_copy(at(src, src_slot, size), at(dst, dst_slot, size), local_sem.at[way])

    def each(way, body, first, last):
        def step(i, carry):
            body(order(me, i, way))
            return carry

        lax.fori_loop(first, last, step, 0)

    load_tiles = pltpu.make_async_copy(tile_ref, tiles, tile_sem.at[0])
    load_batch = pltpu.make_async_copy(batch_ref, batch, tile_sem.at[1])
    barrier = pltpu.get_barrier_semaphore()

    def greet(i, carry):
        pl.semaphore_signal(barrier, inc=1, device_id=(partner(me, i),), device_id_type=MESH)
        return carry

    lax.fori_loop(1, devices, greet, 0)
    load_history(0).start()
    load_history(1).start()
    load_batch.start()
    for b in range(count):
        slot = halo_ref[0, b]
        cluster = slot * count + pull_ref[0, slot]
        mine_smem[0, b] = cluster
        mine_smem[0, 64 + b] = 4 * cluster
        mine_smem[0, 128 + b] = 4 * own_ref[0, b]
    to_vmem = pltpu.make_async_copy(mine_smem, mine, local_sem.at[IDS])
    to_vmem.start()
    spread(feat_ref, feat_wide, lanes, count)
    pl.semaphore_wait(barrier, devices - 1)

    def pack_feat(m):
        feat_send[pl.ds(pl.multiple_of(m * count, count), count), :] = feat_wide[
            pl.ds(m, count, stride=lanes + pad), :
        ].astype(bf16)

    def spread_feat(m):
        pack_feat(m)
        send(at(feat_send, m, count), at(feat_mid, me, count), sems, FEAT_OUT, m)

    each(FEAT_OUT, spread_feat, 1, devices)
    pack_feat(me)
    keep_feat = keep(feat_send, me, feat_mid, me, count, FEAT_OUT)
    keep_feat.start()

    def pack_wide(m):
        wide_send[pl.ds(pl.multiple_of(m * height, height), height), :] = wide[
            pl.ds(m // 32 * rows + m % 32, height, stride=32), :
        ].astype(bf16)

    def spread_hist(m):
        pack_wide(m)
        send_pieces(wide_send, m, hist_mid, me, sems, HIST_OUT, m, (0,))

    def spread_rest(first, last):
        for part in range(1, height // piece):
            each(HIST_OUT, lambda m: send_pieces(wide_send, m, hist_mid, me, sems, HIST_OUT, m, (part,)), first, last)

    load_wide(load_history, 4)
    load_tiles.start()
    pack_wide(me)
    keep_hist = keep(wide_send, me, hist_mid, me, height, HIST_OUT)
    keep_hist.start()
    each(HIST_OUT, spread_hist, 1, 8)
    to_vmem.wait()
    each(IDS, lambda m: send(mine, ids_mid.at[me], sems, IDS, m), 1, devices)
    keep_ids = pltpu.make_async_copy(mine, ids_mid.at[me], local_sem.at[IDS])
    keep_ids.start()
    each(HIST_OUT, spread_hist, 8, devices // 4)
    spread_rest(1, devices // 4)

    load_batch.wait()
    keep_ids.wait()
    wait_all(ids_mid, devices - 1, sems.at[1, IDS])
    to_smem = pltpu.make_async_copy(ids_mid, ids_smem, local_sem.at[IDS])
    to_smem.start()
    to_smem.wait()
    keep_feat.wait()
    wait_all(feat_mid, (devices - 1) * count, sems.at[1, FEAT_OUT])

    widen(feat_mid, feat_wide, 0, rows)

    def pick_feat(d):
        for b in range(count):
            picked[pl.ds(b, 1), :] = feat_wide[pl.ds(batch[b, d], 1), :]
        for b in range(count):
            picked[pl.ds(count + b, 1), :] = feat_wide[pl.ds(ids_smem[d, 0, b], 1), :]
        inputs_send[pl.ds(pl.multiple_of(d * both, both), both), :] = picked[pl.ds(0, both), :].astype(bf16)

    def serve_feat(d):
        pick_feat(d)
        send(at(inputs_send, d, both), at(inputs, me, both), sems, FEAT_IN, d)

    each(FEAT_IN, serve_feat, 1, devices)
    pick_feat(me)
    keep_inputs = keep(inputs_send, me, inputs, me, both, FEAT_IN)
    keep_inputs.start()
    each(HIST_OUT, spread_hist, devices // 4, devices)
    spread_rest(devices // 4, devices)

    keep_inputs.wait()
    wait_all(inputs, (devices - 1) * both, sems.at[1, FEAT_IN])
    load_inputs = functools.partial(load_part, inputs)
    load_inputs(0).start()
    load_inputs(1).start()
    for q in range(2):
        load_inputs(q).wait()
        spread(stage.at[q], wide, both, devices // 2, q * (devices // 2))

    def order_inputs(b, carry):
        given[b] = wide[pl.ds(b, lanes, stride=both + pad), :].astype(bf16)
        return carry

    lax.fori_loop(0, both, order_inputs, 0, unroll=2)
    load_tiles.wait()

    def tile_row(b):
        return jnp.concatenate([tiles[b, 0], tiles[b, 1], tiles[b, 2]], axis=1)

    def first_group(g, carry):
        for k in range(group):
            b = g * group + k
            states = project(
                jnp.concatenate([given[b], given[near[0, b]], given[count + b]], axis=0),
                win_ref[...],
            )
            support[pl.ds(k * lanes, lanes), :] = mix(tile_row(b), states, states[:lanes])
        made = finish(support[...], w_ref[0], 1)
        for k in range(group):
            state[g * group + k] = made[k * lanes : (k + 1) * lanes]
        for q in range(4):
            wide[pl.ds(pl.multiple_of(q * rows + g * span, span), span), :] = made[
                :, q * lanes : (q + 1) * lanes
            ].astype(f32)
        return carry

    lax.fori_loop(0, count // group, first_group, 0)

    keep_hist.wait()
    wait_all(hist_mid, (devices - 1) * height, sems.at[0, HIST_OUT])

    def spread_push(m):
        pack_wide(m)
        send_pieces(wide_send, m, push_mid, me, sems, PUSH_OUT, m, (0,))

    each(PUSH_OUT, spread_push, 1, devices)
    for part in range(1, height // piece):
        each(PUSH_OUT, lambda m: send_pieces(wide_send, m, push_mid, me, sems, PUSH_OUT, m, (part,)), 1, devices)
    pack_wide(me)
    keep_push = keep(wide_send, me, push_mid, me, height, PUSH_OUT)
    keep_push.start()

    wait_all(hist_mid, (devices - 1) * height, sems.at[1, HIST_OUT])
    load_mid = functools.partial(load_part, hist_mid)
    load_mid(0).start()
    load_mid(1).start()
    load_wide(load_mid, 4)

    def pick_wide(dst, d, index):
        for b in range(count):
            picked[pl.ds(4 * b, 4), :] = wide[pl.ds(index(b), 4), :]
        dst[pl.ds(pl.multiple_of(d * height, height), height), :] = picked[...].astype(bf16)

    def pick_halo(d):
        pick_wide(halo_send, d, lambda b: ids_smem[d, 0, 64 + b])

    def serve_halo(d):
        pick_halo(d)
        send_pieces(halo_send, d, halo, me, sems, HIST_IN, d, (0,))

    each(HIST_IN, serve_halo, 1, devices)
    for part in range(1, height // piece):
        each(HIST_IN, lambda d: send_pieces(halo_send, d, halo, me, sems, HIST_IN, d, (part,)), 1, devices)
    pick_halo(me)
    keep_halo = keep(halo_send, me, halo, me, height, HIST_IN)
    keep_halo.start()

    keep_push.wait()
    wait_all(push_mid, (devices - 1) * height, sems.at[1, PUSH_OUT])
    load_push = functools.partial(load_part, push_mid)
    load_push(0).start()
    load_push(1).start()
    wait_all(push_mid, (devices - 1) * height, sems.at[0, PUSH_OUT])
    load_wide(load_push, 4)

    def pick_push(o):
        pick_wide(wide_send, o, lambda p: ids_smem[o, 0, 128 + p])

    def serve_push(o):
        pick_push(o)
        send_pieces(wide_send, o, pushed, me, sems, PUSH_IN, o, (0,))

    each(PUSH_IN, serve_push, 1, devices)
    for part in range(1, height // piece):
        each(PUSH_IN, lambda o: send_pieces(wide_send, o, pushed, me, sems, PUSH_IN, o, (part,)), 1, devices)
    pick_push(me)
    keep_pushed = keep(wide_send, me, pushed, me, height, PUSH_IN)
    keep_pushed.start()

    keep_halo.wait()
    wait_all(halo, (devices - 1) * height, sems.at[1, HIST_IN])
    load_halo = functools.partial(load_part, halo)
    load_halo(0).start()
    load_halo(1).start()
    load_wide(load_halo, 4)

    def halo_block(b):
        return jnp.concatenate(
            [
                jnp.concatenate(
                    [wide[pl.ds(q * rows + 4 * b + i, 32, stride=height), :] for i in range(4)], axis=0
                )
                for q in range(4)
            ],
            axis=1,
        ).astype(bf16)

    def write(g, slot):
        return pltpu.make_async_copy(
            ready.at[slot], second.at[pl.ds(pl.multiple_of(g * span, span), span)], out_sem.at[slot]
        )

    def second_pair(pair, carry):
        for slot in range(2):
            g = pair * 2 + slot
            for k in range(group):
                b = g * group + k
                initial = project(given[b], win_ref[...])
                states = jnp.concatenate([state[b], state[near[0, b]], halo_block(b)], axis=0)
                support[pl.ds(k * lanes, lanes), :] = mix(tile_row(b), states, initial)
            made = finish(support[...], w_ref[1], 2)

            @pl.when(pair > 0)
            def _():
                write(g - 2, slot).wait()

            ready[slot] = made
            write(g, slot).start()
        return carry

    lax.fori_loop(0, count // group // 2, second_pair, 0)
    for slot in range(2):
        write(count // group - 2 + slot, slot).wait()

    keep_pushed.wait()
    wait_all(pushed, (devices - 1) * height, sems.at[1, PUSH_IN])
    wait_all(ids_mid, devices - 1, sems.at[0, IDS])
    wait_all(feat_mid, (devices - 1) * count, sems.at[0, FEAT_OUT])
    wait_all(inputs, (devices - 1) * both, sems.at[0, FEAT_IN])
    wait_all(halo, (devices - 1) * height, sems.at[0, HIST_IN])
    wait_all(pushed, (devices - 1) * height, sems.at[0, PUSH_IN])


def run_step(batch, own, near, halo, pull, features, history, tiles, w_in, w_layers):
    anywhere = pl.BlockSpec(memory_space=pl.ANY)
    smem = pl.BlockSpec(memory_space=pltpu.SMEM)
    vmem = pl.BlockSpec(memory_space=pltpu.VMEM)
    shape = lambda *dims: jax.ShapeDtypeStruct(dims, bf16)
    sliced = shape(4 * rows, lanes)
    return pl.pallas_call(
        step_body,
        in_specs=[anywhere, smem, smem, smem, smem, vmem, anywhere, anywhere, vmem, vmem],
        out_specs=[anywhere] * 6,
        out_shape=[shape(rows, 4 * lanes), shape(2 * rows, lanes), sliced, sliced, sliced, sliced],
        scratch_shapes=[
            pltpu.SMEM((count, devices), jnp.int32),
            pltpu.SMEM((1, 2 * lanes), jnp.int32),
            pltpu.VMEM((1, 2 * lanes), jnp.int32),
            pltpu.VMEM((devices, 1, 2 * lanes), jnp.int32),
            pltpu.SMEM((devices, 1, 2 * lanes), jnp.int32),
            pltpu.VMEM(((count + 1) * (lanes + pad), lanes), f32),
            pltpu.VMEM((4 * rows + 2 * lanes, lanes), f32),
            pltpu.VMEM((2, rows, lanes), bf16),
            pltpu.VMEM((rows, lanes), bf16),
            pltpu.VMEM((rows, lanes), bf16),
            pltpu.VMEM((2 * rows, lanes), bf16),
            pltpu.VMEM((both, lanes, lanes), bf16),
            pltpu.VMEM((4 * rows, lanes), bf16),
            pltpu.VMEM((4 * rows, lanes), bf16),
            pltpu.VMEM((count, lanes, 4 * lanes), bf16),
            pltpu.VMEM((span, 4 * lanes), f32),
            pltpu.VMEM((count, 3, lanes, lanes), bf16),
            pltpu.VMEM((2, span, 4 * lanes), bf16),
            pltpu.VMEM((height, lanes), f32),
            pltpu.SemaphoreType.DMA((2, WAYS)),
            pltpu.SemaphoreType.DMA((WAYS,)),
            pltpu.SemaphoreType.DMA((2,)),
            pltpu.SemaphoreType.DMA((2,)),
            pltpu.SemaphoreType.DMA((2,)),
        ],
        compiler_params=pltpu.CompilerParams(
            vmem_limit_bytes=vmem_bytes, collective_id=1, has_side_effects=True
        ),
        cost_estimate=pl.CostEstimate(flops=14_000_000_000, bytes_accessed=100_000_000, transcendentals=0),
    )(batch, own, near, halo, pull, features, history, tiles, w_in, w_layers)


def place_body(pushed, second, fresh, result, wide):
    result[...] = second[...]
    spread(pushed, wide, height, 32)

    def move(a, carry):
        fresh[pl.ds(pl.multiple_of(a * 32, 32), 32), :] = wide[
            pl.ds(a, 32, stride=height + pad), :
        ].astype(bf16)
        return carry

    lax.fori_loop(0, height, move, 0, unroll=8)


def place(pushed, second):
    full = jax.ShapeDtypeStruct((rows, 4 * lanes), bf16)
    quarter = pl.BlockSpec((rows // 4, 4 * lanes), lambda q: (q, 0))
    return pl.pallas_call(
        place_body,
        grid=(4,),
        in_specs=[pl.BlockSpec((rows, lanes), lambda q: (q, 0)), quarter],
        out_specs=[pl.BlockSpec((rows, lanes), lambda q: (0, q)), quarter],
        out_shape=[full, full],
        scratch_shapes=[pltpu.VMEM((33 * (height + pad), lanes), f32)],
        compiler_params=pltpu.CompilerParams(vmem_limit_bytes=vmem_bytes),
        cost_estimate=pl.CostEstimate(flops=0, bytes_accessed=40_000_000, transcendentals=0),
    )(pushed, second)


def own_places(batch):
    spot = jnp.arange(batch.size, dtype=jnp.int32).reshape(batch.shape)[:, :, None]
    cluster = lax.axis_index("dev") * count + jnp.arange(count, dtype=jnp.int32)
    return jnp.sum(jnp.where(batch[:, :, None] == cluster, spot, 0), axis=(0, 1)).reshape(1, count)


def local(features, history, batch_clusters, pull_list, halo_ref, in_ref, tiles, w_in, w_layers):
    second, _, _, _, _, pushed = run_step(
        batch_clusters.T, own_places(batch_clusters), in_ref, halo_ref, pull_list,
        features, history, tiles, w_in, w_layers,
    )
    fresh, second_layer = place(pushed, second)
    return (second_layer, fresh)


def solution(mesh):
    placed = (
        P("dev", None),
        P("dev", None),
        P(),
        P("dev", None),
        P("dev", None),
        P("dev", None),
        P("dev", None, None, None),
        P(),
        P(),
    )
    return jax.shard_map(
        local,
        mesh=mesh,
        in_specs=placed,
        out_specs=(P("dev", None), P("dev", None)),
        check_vma=False,
    )
```
